128 devices in a mesh: dp: 64 (over z, x, y), mp: 2 (over core).
Axes of the slice: x: 4, y: 4, z: 4, core: 2. Of those that a mesh axis runs over, the one named last changes fastest.
Arguments:
- tokens: bfloat16 [32768, 1024], P('dp'), may hold values from -6 to 6
- sample_owner: int32 [512], P('dp'), may hold values from 0 to 63, as said below
- sample_slot: int32 [512], P('dp'), may hold values from 0 to 15
- teacher_cache: bfloat16 [1024, 64, 3200], P('dp', None, 'mp'), may hold values from -6 to 6
- fc_weight: bfloat16 [1024, 4096], P(None, 'mp'), may hold values from -0.1875 to 0.1875
- proj_weight: bfloat16 [4096, 1024], P('mp'), may hold values from -0.09375 to 0.09375
- head_weight: bfloat16 [1024, 3200], P(None, 'mp'), may hold values from -0.1875 to 0.1875
Outputs:
- fc_grad: float32 [1024, 4096], P('dp', 'mp')
- proj_grad: float32 [4096, 1024], P('mp', 'dp')
- head_grad: float32 [1024, 3200], P('dp', 'mp')
The draws below stay inside these ranges and needn't reach their ends.
Inputs may be any that keep to these rules, and one draw needn't show every extreme that they name: `sample_owner`: the 8 samples of the index d of dp name 8 different owners, among them (d - 1) mod 64 and (d + 32) mod 64; some owners are named far more often than others.
All inputs are finite; a program needn't handle non-finite values.
Results may differ from the reference program's by a relative error of at most 0.01.
Values may be sent and summed in bfloat16 or wider, within the bound.
No kernel may reach another device: no remote copies, remote signals or barrier semaphores. Data moves between devices by JAX's collectives and lax.ppermute only.
A program may use at most 128 MiB of HBM per device.

```python
import math
import jax
import jax.numpy as jnp
from jax import lax

D = 1024
FF = 4096
FEAT = 3200
PATCH_S = 64
B_DEV = 8
CACHE_DEV = 16
SAMPLES = 512
TOKENS = 32768
CACHE = 1024
N_DP = 64
N_MP = 2


def draw_sample_owner(key, part):
    devices = SAMPLES // B_DEV
    key_pop, key_jitter = jax.random.split(jax.random.fold_in(key, 11))
    popular = jax.random.randint(key_pop, (devices,), 0, 4) * 262144
    jitter = jax.random.randint(key_jitter, (devices, devices), 0, 1048576)
    scores = (popular[None, :] + jitter) * devices + jnp.arange(devices, dtype=jnp.int32)[None, :]
    rows = jnp.arange(devices, dtype=jnp.int32)[:, None]
    columns = jnp.arange(devices, dtype=jnp.int32)[None, :]
    prev_owner = (rows + devices - 1) % devices
    far_owner = (rows + devices // 2) % devices
    scores = jnp.where(columns == prev_owner, jnp.int32(1073741825), scores)
    scores = jnp.where(columns == far_owner, jnp.int32(1073741824), scores)
    _, chosen = lax.top_k(scores, B_DEV)
    return chosen.reshape(SAMPLES).astype(jnp.int32)


def place_ends(entries, key, smallest, high):
    place = [jax.random.randint(jax.random.fold_in(key, axis), (), 0, length) for axis, length in enumerate(entries.shape)]
    longest = entries.shape.index(max(entries.shape))
    next_to = place[:longest] + [(place[longest] + 1) % entries.shape[longest]] + place[longest + 1:]
    return entries.at[tuple(place)].set(smallest).at[tuple(next_to)].set(high)


def block_levels(own_key, extent, shards, least, largest):
    factor_of = 1.0
    for axis_at, shards_of in shards:
        steps = jax.random.uniform(jax.random.fold_in(jax.random.fold_in(own_key, 6), axis_at), (shards_of,), jnp.float32, least / len(shards), largest / len(shards))
        factor_of = factor_of * jnp.repeat(jnp.exp(steps), extent[axis_at] // shards_of).reshape((-1,) + (1,) * (len(extent) - 1 - axis_at))
    return factor_of


def noise(rng, dims, scale, reach, cuts=(), kind=jnp.bfloat16):
    factor_of = block_levels(rng, dims, cuts, -0.22, 0.18) if cuts else 1.0
    result = jax.random.normal(rng, dims, jnp.float32) * scale * factor_of
    return jnp.minimum(jnp.maximum(result, -reach), reach).astype(kind)


def setup_inputs(seed: int = 0) -> dict:
    arg_keys = jax.random.split(jax.random.key(seed), 8)
    tokens = noise(arg_keys[0], (TOKENS, D), 1.0, 6.0, ((0, 64),))
    sample_owner = draw_sample_owner(jax.random.fold_in(arg_keys[7], 71), 0)
    sample_slot = place_ends(jax.random.randint(arg_keys[2], (SAMPLES,), 0, CACHE_DEV), jax.random.fold_in(arg_keys[2], 1), 0, CACHE_DEV - 1).astype(jnp.int32)
    teacher_cache = noise(arg_keys[3], (CACHE, PATCH_S, FEAT), 1.0, 6.0, ((0, 64), (2, 2)))
    fc_weight = noise(arg_keys[4], (D, FF), D ** -0.5, 0.1875, ((1, 2),))
    proj_weight = noise(arg_keys[5], (FF, D), FF ** -0.5, 0.09375, ((0, 2),))
    head_weight = noise(arg_keys[6], (D, FEAT), D ** -0.5, 0.1875, ((1, 2),))
    return {"tokens": tokens, "sample_owner": sample_owner, "sample_slot": sample_slot, "teacher_cache": teacher_cache, "fc_weight": fc_weight, "proj_weight": proj_weight, "head_weight": head_weight}


gelu_coef = 0.7978845608

def normalize(values):
    values = values.astype(jnp.float32)
    center = lax.optimization_barrier(jnp.mean(values, axis=-1, keepdims=True))
    spread = lax.optimization_barrier(jnp.mean((values - center) ** 2, axis=-1, keepdims=True))
    inverse = 1.0 / jnp.sqrt(spread + 1e-06)
    return ((values - center) * inverse, inverse)

def gelu_tanh(values):
    return 0.5 * values * (1.0 + jnp.tanh(gelu_coef * (values + 0.044715 * values ** 3)))

def gelu_slope(values):
    inner = jnp.tanh(gelu_coef * (values + 0.044715 * values ** 3))
    return 0.5 * (1.0 + inner) + 0.5 * values * (1.0 - inner * inner) * gelu_coef * (1.0 + 3.0 * 0.044715 * values * values)

def rounded(values):
    lowered = lax.optimization_barrier(values.astype(jnp.bfloat16))
    return lowered.astype(jnp.float32)

def reference(tokens, sample_owner, sample_slot, teacher_cache, fc_weight, proj_weight, head_weight):
    tok_rows = B_DEV * PATCH_S
    loss_scale = 1.0 / math.sqrt(TOKENS)
    half_hidden = FF // N_MP
    half_feat = FEAT // N_MP

    def block_step(totals, inputs):
        tok_block, owner_ids, slot_ids = inputs
        block_index = (owner_ids * CACHE_DEV + slot_ids).astype(jnp.int32)
        target = jnp.take(teacher_cache, block_index, axis=0).reshape(tok_rows, FEAT)
        normal_in, _ = normalize(tok_block)
        normed_in = normal_in.astype(jnp.bfloat16)
        pre_act = jnp.dot(normed_in, fc_weight, preferred_element_type=jnp.float32)
        act_out = gelu_tanh(pre_act).astype(jnp.bfloat16)
        mlp_out = jnp.zeros((tok_rows, D), jnp.float32)
        for group in range(N_MP):
            lower = group * half_hidden
            mlp_out = mlp_out + rounded(jnp.dot(act_out[:, lower:lower + half_hidden], proj_weight[lower:lower + half_hidden], preferred_element_type=jnp.float32))
        hidden = tok_block.astype(jnp.float32) + mlp_out
        normal_out, inverse = normalize(hidden)
        normed_out = normal_out.astype(jnp.bfloat16)
        pred = jnp.dot(normed_out, head_weight, preferred_element_type=jnp.float32)
        err_scaled = ((pred - target.astype(jnp.float32)) * loss_scale).astype(jnp.bfloat16)
        head_grad = jnp.dot(normed_out.T, err_scaled, preferred_element_type=jnp.float32)
        grad_norm = jnp.zeros((tok_rows, D), jnp.float32)
        for group in range(N_MP):
            lower = group * half_feat
            grad_norm = grad_norm + rounded(jnp.dot(err_scaled[:, lower:lower + half_feat], head_weight[:, lower:lower + half_feat].T, preferred_element_type=jnp.float32))
        grad_hidden = inverse * (grad_norm - lax.optimization_barrier(jnp.mean(grad_norm, axis=-1, keepdims=True)) - normal_out * lax.optimization_barrier(jnp.mean(grad_norm * normal_out, axis=-1, keepdims=True)))
        grad_hidden = grad_hidden.astype(jnp.bfloat16)
        proj_grad = jnp.dot(act_out.T, grad_hidden, preferred_element_type=jnp.float32)
        grad_act = jnp.dot(grad_hidden, proj_weight.T, preferred_element_type=jnp.float32)
        grad_pre = (grad_act * gelu_slope(pre_act)).astype(jnp.bfloat16)
        fc_grad = jnp.dot(normed_in.T, grad_pre, preferred_element_type=jnp.float32)
        return ((totals[0] + fc_grad, totals[1] + proj_grad, totals[2] + head_grad), None)
    start = (jnp.zeros((D, FF), jnp.float32), jnp.zeros((FF, D), jnp.float32), jnp.zeros((D, FEAT), jnp.float32))
    inputs = (tokens.reshape(N_DP, tok_rows, D), sample_owner.reshape(N_DP, B_DEV), sample_slot.reshape(N_DP, B_DEV))
    totals, _ = lax.scan(block_step, start, inputs)
    return (totals[0], totals[1], totals[2])
```

```python
import math

import jax
import jax.numpy as jnp
from jax import lax
from jax.sharding import Mesh, PartitionSpec as P

gelu_coef = 0.7978845608
DP = ("z", "x", "y")
SIDE = 4
RING = list(range(SIDE))


def normalize(values):
    values = values.astype(jnp.float32)
    center = jnp.mean(values, axis=-1, keepdims=True)
    spread = jnp.mean((values - center) ** 2, axis=-1, keepdims=True)
    inverse = 1.0 / jnp.sqrt(spread + 1e-06)
    return ((values - center) * inverse, inverse)


def gelu_tanh(values):
    return 0.5 * values * (1.0 + jnp.tanh(gelu_coef * (values + 0.044715 * values**3)))


def gelu_slope(values):
    inner = jnp.tanh(gelu_coef * (values + 0.044715 * values**3))
    return 0.5 * (1.0 + inner) + 0.5 * values * (1.0 - inner * inner) * gelu_coef * (
        1.0 + 3.0 * 0.044715 * values * values
    )


def dot(a, b, ca, cb):
    return lax.dot_general(a, b, (((ca,), (cb,)), ((), ())), preferred_element_type=jnp.float32)


def gather_line(values, axis):
    parts = [values] + [
        lax.ppermute(values, axis, [((t + m) % SIDE, t) for t in RING]) for m in (1, 2, 3)
    ]
    around = jnp.stack(parts + parts)
    return lax.dynamic_slice_in_dim(around, SIDE - lax.axis_index(axis), SIDE, 0)


def pair_sum(part):
    return part.astype(jnp.float32) + lax.ppermute(part, "mp", [(0, 1), (1, 0)]).astype(jnp.float32)


def first_mate(t, core):
    return t ^ 1 if core == 0 else 3 - t


def halve(blocks, dim, axis, last):
    t, core = lax.axis_index(axis), lax.axis_index("mp")
    near, far = jnp.bitwise_xor(t, 1), 3 - t
    mate_1 = jnp.where(core == 0, near, far)
    mate_2 = jnp.where(core == 0, far, near)
    across = jnp.bitwise_xor(t, 2)

    def at(slot):
        return lax.dynamic_slice_in_dim(blocks, slot, 1, dim)

    step_1 = [(p * 2 + c, first_mate(p, c) * 2 + c) for p in RING for c in (0, 1)]
    step_2 = [(p * 2 + c, first_mate(p, 1 - c) * 2 + c) for p in RING for c in (0, 1)]
    sent = jnp.concatenate([at(mate_1), at(across)], 0)
    came = lax.ppermute(sent, (axis, "mp"), step_1)
    lead = blocks.shape[0] if dim else 1
    kept = at(mate_2).astype(jnp.float32) + came[lead:].astype(jnp.float32)
    came_2 = lax.ppermute(kept.astype(jnp.bfloat16), (axis, "mp"), step_2)
    mine = at(t).astype(jnp.float32) + came[:lead].astype(jnp.float32)
    total = mine + came_2.astype(jnp.float32)
    return total if last else total.astype(jnp.bfloat16)


def scatter_sum(grad, order):
    cols = grad.shape[1]
    blocks = grad.astype(jnp.bfloat16).reshape(SIDE, SIDE, SIDE, 16, cols)
    for step, axis in enumerate(order):
        blocks = halve(blocks, DP.index(axis), axis, step == 2)
    return blocks.reshape(16, cols)


def per_device(
    tokens, sample_owner, sample_slot, teacher_cache, fc_weight, proj_weight, head_weight
):
    tok_rows, width = tokens.shape
    slots, patches, feats = teacher_cache.shape
    samples = tok_rows // patches
    devices = SIDE**3
    loss_scale = 1.0 / math.sqrt(tok_rows * devices)
    spread = lax.all_to_all(
        teacher_cache.transpose(1, 0, 2), DP, split_axis=0, concat_axis=0, tiled=True
    ).reshape(devices * slots, feats)
    wanted = sample_owner * slots + sample_slot
    for axis in ("y", "x", "z"):
        wanted = gather_line(wanted, axis).reshape(-1)
    chosen = (wanted[:, None] == jnp.arange(devices * slots, dtype=jnp.int32)[None, :]).astype(
        jnp.bfloat16
    )
    rows_out = dot(chosen, spread, 1, 0).astype(jnp.bfloat16).reshape(devices, samples, feats)
    target = lax.all_to_all(rows_out, DP, split_axis=0, concat_axis=0, tiled=True).reshape(
        tok_rows, feats
    )
    tokens = tokens.reshape(samples, patches, width).transpose(1, 0, 2).reshape(tok_rows, width)
    normal_in, _ = normalize(tokens)
    normed_in = normal_in.astype(jnp.bfloat16)
    pre_act = dot(normed_in, fc_weight, 1, 0)
    act_out = gelu_tanh(pre_act).astype(jnp.bfloat16)
    mlp_out = pair_sum(dot(act_out, proj_weight, 1, 0).astype(jnp.bfloat16))
    hidden = tokens.astype(jnp.float32) + mlp_out
    normal_out, inverse = normalize(hidden)
    normed_out = normal_out.astype(jnp.bfloat16)
    pred = dot(normed_out, head_weight, 1, 0)
    err_scaled = ((pred - target.astype(jnp.float32)) * loss_scale).astype(jnp.bfloat16)
    head_grad = dot(normed_out, err_scaled, 0, 0)
    grad_norm = pair_sum(dot(err_scaled, head_weight, 1, 1).astype(jnp.bfloat16))
    grad_hidden = inverse * (
        grad_norm
        - jnp.mean(grad_norm, axis=-1, keepdims=True)
        - normal_out * jnp.mean(grad_norm * normal_out, axis=-1, keepdims=True)
    )
    grad_hidden = grad_hidden.astype(jnp.bfloat16)
    proj_grad = dot(grad_hidden, act_out, 0, 0)
    grad_act = dot(grad_hidden, proj_weight, 1, 1)
    grad_pre = (grad_act * gelu_slope(pre_act)).astype(jnp.bfloat16)
    fc_grad = dot(normed_in, grad_pre, 0, 0)
    head_shard = scatter_sum(head_grad, ("z", "x", "y"))
    proj_shard = scatter_sum(proj_grad, ("x", "y", "z"))
    fc_shard = scatter_sum(fc_grad, ("y", "z", "x"))
    return (fc_shard, proj_shard.T, head_shard)


def solution(mesh):
    torus = Mesh(mesh.devices.reshape(SIDE, SIDE, SIDE, 2), (*DP, "mp"))
    in_specs = (
        P(DP, None),
        P(DP),
        P(DP),
        P(DP, None, "mp"),
        P(None, "mp"),
        P("mp", None),
        P(None, "mp"),
    )
    out_specs = (P(DP, "mp"), P("mp", DP), P(DP, "mp"))
    return jax.shard_map(
        per_device, mesh=torus, in_specs=in_specs, out_specs=out_specs, check_vma=False
    )
```

```python
import math

import jax
import jax.numpy as jnp
from jax import lax
from jax.experimental import pallas as pl
from jax.experimental.pallas import tpu as pltpu
from jax.sharding import Mesh, PartitionSpec as P

gelu_coef = 0.7978845608
DP = ("z", "x", "y")
SIDE = 4
RING = list(range(SIDE))
TILE = 16


def normalize(values):
    values = values.astype(jnp.float32)
    center = jnp.mean(values, axis=-1, keepdims=True)
    spread = jnp.mean((values - center) ** 2, axis=-1, keepdims=True)
    inverse = 1.0 / jnp.sqrt(spread + 1e-06)
    return ((values - center) * inverse, inverse)


def dot(a, b, ca=1, cb=0):
    return lax.dot_general(a, b, (((ca,), (cb,)), ((), ())), preferred_element_type=jnp.float32)


def stored(*values):
    return lax.optimization_barrier(values)


def swap_cores(part):
    return lax.ppermute(part, "mp", [(0, 1), (1, 0)])


def spread_kernel(block_ref, note_ref, out_ref):
    slots, patches, feats = block_ref.shape
    rows = slots * patches
    to = lax.broadcasted_iota(jnp.int32, (rows, rows), 0)
    source = lax.broadcasted_iota(jnp.int32, (rows, rows), 1)
    pick = (source == (to % slots) * patches + to // slots).astype(jnp.bfloat16)
    moved = dot(pick, block_ref[...].reshape(rows, feats)).astype(jnp.bfloat16)
    out_ref[:, :, :feats] = moved.reshape(patches, slots, feats)
    note = note_ref[...]
    out_ref[:, :, feats:] = jnp.broadcast_to(note[None], (patches, *note.shape))


def to_patch_major(teacher_cache, note):
    slots, patches, feats = teacher_cache.shape
    wide = feats + note.shape[1]
    return pl.pallas_call(
        spread_kernel,
        grid=(patches // TILE,),
        in_specs=[
            pl.BlockSpec((slots, TILE, feats), lambda i: (0, i, 0)),
            pl.BlockSpec(note.shape, lambda i: (0, 0)),
        ],
        out_specs=pl.BlockSpec((TILE, slots, wide), lambda i: (i, 0, 0)),
        out_shape=jax.ShapeDtypeStruct((patches, slots, wide), jnp.bfloat16),
        compiler_params=pltpu.CompilerParams(vmem_limit_bytes=32 * 2**20),
    )(teacher_cache, note)


def mate(t, core, step):
    return t ^ 1 if core == step else 3 - t


def row_order(order):
    rows = jnp.arange(SIDE**3 * TILE, dtype=jnp.int32)
    core = lax.axis_index("mp")
    source = rows % TILE
    for place, axis in enumerate(order):
        slot = rows // (SIDE ** (2 - place) * TILE) % SIDE
        t = lax.axis_index(axis)
        near, far = t ^ 1, 3 - t
        first = jnp.where(core == 0, near, far)
        second = jnp.where(core == 0, far, near)
        digit = jnp.where(
            slot == 0, t ^ 2, jnp.where(slot == 1, first, jnp.where(slot == 2, second, t))
        )
        source = source + digit * (SIDE ** (2 - DP.index(axis)) * TILE)
    return source


def arranger(order):
    source = row_order(order)
    picks = (source[:, None] == jnp.arange(source.shape[0], dtype=jnp.int32)[None, :]).astype(
        jnp.bfloat16
    )
    half = source.shape[0] // 2
    return picks[:half], picks[half:]


def scatter_sum(sent, kept, order):
    for axis in order:
        for step in (0, 1):
            pairs = [(p * 2 + c, mate(p, c, step) * 2 + c) for p in RING for c in (0, 1)]
            came = lax.ppermute(sent, (axis, "mp"), pairs)
            half = kept.shape[0] // 2
            if half < TILE:
                return kept.astype(jnp.float32) + came.astype(jnp.float32)
            sent, kept = (
                (kept[part].astype(jnp.float32) + came[part].astype(jnp.float32)).astype(
                    jnp.bfloat16
                )
                for part in (slice(0, half), slice(half, None))
            )
    return None


def per_device(
    tokens, sample_owner, sample_slot, teacher_cache, fc_weight, proj_weight, head_weight
):
    tok_rows, width = tokens.shape
    slots, patches, feats = teacher_cache.shape
    samples = tok_rows // patches
    devices = SIDE**3
    wide = -(-feats // 128) * 128
    loss_scale = 1.0 / math.sqrt(tok_rows * devices)
    note = jnp.stack([sample_owner, sample_slot], 1).astype(jnp.bfloat16)
    note = jnp.pad(note, ((0, slots - samples), (0, wide - feats - 2)))
    spread = lax.all_to_all(
        to_patch_major(teacher_cache, note), DP, split_axis=0, concat_axis=0, tiled=True
    )
    asked = spread[:, :samples, feats : feats + 2].astype(jnp.int32)
    wanted = (asked[:, :, 0] * slots + asked[:, :, 1]).reshape(devices * samples)
    chosen = (wanted[:, None] == jnp.arange(devices * slots, dtype=jnp.int32)[None, :]).astype(
        jnp.bfloat16
    )
    rows_out = dot(chosen, spread.reshape(devices * slots, wide)).astype(jnp.bfloat16)
    target = lax.all_to_all(
        rows_out.reshape(devices, samples, wide), DP, split_axis=0, concat_axis=0, tiled=True
    ).reshape(tok_rows, wide)

    tokens = tokens.reshape(samples, patches, width).transpose(1, 0, 2).reshape(tok_rows, width)
    (tokens,) = stored(tokens)
    normal_in, _ = normalize(tokens)
    (normed_in,) = stored(normal_in.astype(jnp.bfloat16))
    pre_act = dot(normed_in, fc_weight)
    inner = jnp.tanh(gelu_coef * (pre_act + 0.044715 * pre_act**3))
    slope = 0.5 * (1.0 + inner) + 0.5 * pre_act * (1.0 - inner * inner) * gelu_coef * (
        1.0 + 3.0 * 0.044715 * pre_act * pre_act
    )
    act_out, slope = stored((0.5 * pre_act * (1.0 + inner)).astype(jnp.bfloat16), slope)
    (mlp_part,) = stored(dot(act_out, proj_weight).astype(jnp.bfloat16))
    mlp_out = mlp_part.astype(jnp.float32) + swap_cores(mlp_part).astype(jnp.float32)
    hidden = tokens.astype(jnp.float32) + mlp_out
    normal_out, inverse = normalize(hidden)
    normal_out, normed_out, inverse = stored(normal_out, normal_out.astype(jnp.bfloat16), inverse)
    head_wide = jnp.pad(head_weight, ((0, 0), (0, wide - feats)))
    (head_wide,) = stored(head_wide.T)
    (pred,) = stored(dot(normed_out, head_wide, 1, 1))

    orders = {"head": ("z", "x", "y"), "proj": ("x", "y", "z"), "fc": ("y", "z", "x")}
    picks = {name: stored(*arranger(order)) for name, order in orders.items()}

    def turned(name, values):
        return stored(*(dot(pick, values, 1, 1).astype(jnp.bfloat16) for pick in picks[name]))

    head_left = turned("head", normed_out)
    fc_left = turned("fc", normed_in)

    (err_scaled,) = stored(
        ((pred - target.astype(jnp.float32)) * loss_scale).astype(jnp.bfloat16)
    )
    (grad_part,) = stored(dot(err_scaled, head_wide).astype(jnp.bfloat16))
    grad_norm = grad_part.astype(jnp.float32) + swap_cores(grad_part).astype(jnp.float32)
    head_shard = scatter_sum(
        *stored(*(dot(left, err_scaled).astype(jnp.bfloat16) for left in head_left)),
        orders["head"],
    )
    grad_hidden = inverse * (
        grad_norm
        - jnp.mean(grad_norm, axis=-1, keepdims=True)
        - normal_out * jnp.mean(grad_norm * normal_out, axis=-1, keepdims=True)
    )
    (grad_hidden,) = stored(grad_hidden.astype(jnp.bfloat16))
    proj_left = turned("proj", grad_hidden)
    proj_shard = scatter_sum(
        *stored(*(dot(left, act_out).astype(jnp.bfloat16) for left in proj_left)),
        orders["proj"],
    )
    (grad_pre,) = stored(
        (dot(grad_hidden, proj_weight, 1, 1) * slope).astype(jnp.bfloat16)
    )
    fc_shard = scatter_sum(
        *stored(*(dot(left, grad_pre).astype(jnp.bfloat16) for left in fc_left)), orders["fc"]
    )
    return (fc_shard, proj_shard.T, head_shard[:, :feats])


def solution(mesh):
    torus = Mesh(mesh.devices.reshape(SIDE, SIDE, SIDE, 2), (*DP, "mp"))
    in_specs = (
        P(DP, None),
        P(DP),
        P(DP),
        P(DP, None, "mp"),
        P(None, "mp"),
        P("mp", None),
        P(None, "mp"),
    )
    out_specs = (P(DP, "mp"), P("mp", DP), P(DP, "mp"))
    return jax.shard_map(
        per_device, mesh=torus, in_specs=in_specs, out_specs=out_specs, check_vma=False
    )
```

```python
import functools
import math

import jax
import jax.numpy as jnp
from jax import lax
from jax.experimental import pallas as pl
from jax.experimental.pallas import tpu as pltpu
from jax.sharding import Mesh, PartitionSpec as P

gelu_coef = 0.7978845608
DP = ("z", "x", "y")
SIDE = 4
RING = list(range(SIDE))
TILE = 16


def normalize(values):
    values = values.astype(jnp.float32)
    center = jnp.mean(values, axis=-1, keepdims=True)
    spread = jnp.mean((values - center) ** 2, axis=-1, keepdims=True)
    inverse = 1.0 / jnp.sqrt(spread + 1e-06)
    return ((values - center) * inverse, inverse)


def dot(a, b, ca=1, cb=0):
    return lax.dot_general(a, b, (((ca,), (cb,)), ((), ())), preferred_element_type=jnp.float32)


def stored(*values):
    return lax.optimization_barrier(values)


def swap_cores(part):
    return lax.ppermute(part, "mp", [(0, 1), (1, 0)])


def spread_kernel(scale, block_ref, weight_ref, rows_ref, product_ref):
    slots, patches, feats = block_ref.shape
    rows = slots * patches
    to = lax.broadcasted_iota(jnp.int32, (rows, rows), 0)
    source = lax.broadcasted_iota(jnp.int32, (rows, rows), 1)
    pick = (source == (to % slots) * patches + to // slots).astype(jnp.bfloat16)
    moved = dot(pick, block_ref[...].reshape(rows, feats)).astype(jnp.bfloat16)
    rows_ref[:, :feats] = moved
    rows_ref[:, feats:] = jnp.zeros((rows, rows_ref.shape[1] - feats), jnp.bfloat16)
    product = (dot(moved, weight_ref[...]) * scale).astype(jnp.bfloat16)
    half = product.shape[1] // 2
    product_ref[0] = product[:, :half]
    product_ref[1] = product[:, half:]


def patch_major(teacher_cache, weight, scale, wide):
    slots, patches, feats = teacher_cache.shape
    width = weight.shape[1]
    return pl.pallas_call(
        functools.partial(spread_kernel, scale),
        grid=(patches // TILE,),
        in_specs=[
            pl.BlockSpec((slots, TILE, feats), lambda i: (0, i, 0)),
            pl.BlockSpec((feats, width), lambda i: (0, 0)),
        ],
        out_specs=[
            pl.BlockSpec((TILE * slots, wide), lambda i: (i, 0)),
            pl.BlockSpec((2, TILE * slots, width // 2), lambda i: (0, i, 0)),
        ],
        out_shape=[
            jax.ShapeDtypeStruct((patches * slots, wide), jnp.bfloat16),
            jax.ShapeDtypeStruct((2, patches * slots, width // 2), jnp.bfloat16),
        ],
        compiler_params=pltpu.CompilerParams(vmem_limit_bytes=40 * 2**20),
    )(teacher_cache, weight)


def mate(t, core, step):
    return t ^ 1 if core == step else 3 - t


def row_source():
    rows = jnp.arange(SIDE**3 * TILE, dtype=jnp.int32)
    core = lax.axis_index("mp")
    source = rows % TILE
    for place, axis in enumerate(DP):
        step = SIDE ** (2 - place) * TILE
        slot = rows // step % SIDE
        t = lax.axis_index(axis)
        near, far = t ^ 1, 3 - t
        first = jnp.where(core == 0, near, far)
        second = jnp.where(core == 0, far, near)
        digit = jnp.where(
            slot == 0, t ^ 2, jnp.where(slot == 1, first, jnp.where(slot == 2, second, t))
        )
        source = source + digit * step
    return source


def one_hot(source, size):
    return (source[:, None] == jnp.arange(size, dtype=jnp.int32)[None, :]).astype(jnp.bfloat16)


def halves(values, axis):
    dim = DP.index(axis)
    half = values.shape[dim] // 2
    return (
        lax.slice_in_dim(values, 0, half, axis=dim),
        lax.slice_in_dim(values, half, 2 * half, axis=dim),
    )


def first_halves(grad, order):
    return (*halves(grad.reshape(SIDE, SIDE, SIDE, TILE, grad.shape[1]), order[0]), order)


def exchange(streams, turn):
    step = turn % 2
    pairs = [(p * 2 + c, mate(p, c, step) * 2 + c) for p in RING for c in (0, 1)]
    came = [lax.ppermute(sent, (order[turn // 2], "mp"), pairs) for sent, _, order in streams]
    totals = [
        kept.astype(jnp.float32) + part.astype(jnp.float32)
        for (_, kept, _), part in zip(streams, came)
    ]
    if turn == 5:
        return [total.reshape(TILE, -1) for total in totals]
    return [
        (*halves(total.astype(jnp.bfloat16), order[(turn + 1) // 2]), order)
        for total, (_, _, order) in zip(totals, streams)
    ]


def together(streams, *others):
    flat = stored(*(x for sent, kept, _ in streams for x in (sent, kept)), *others)
    count = 2 * len(streams)
    joined = [
        (flat[2 * i], flat[2 * i + 1], order) for i, (_, _, order) in enumerate(streams)
    ]
    return joined, flat[count:]


def per_device(
    tokens, sample_owner, sample_slot, teacher_cache, fc_weight, proj_weight, head_weight
):
    tok_rows, width = tokens.shape
    slots, patches, feats = teacher_cache.shape
    samples = tok_rows // patches
    devices = SIDE**3
    half = width // 2
    wide = -(-feats // 128) * 128
    loss_scale = 1.0 / math.sqrt(tok_rows * devices)
    core = lax.axis_index("mp")

    teacher_rows, products = patch_major(teacher_cache, head_weight.T, loss_scale, wide)
    own = lax.dynamic_index_in_dim(products, core, 0, keepdims=False)
    partner = lax.dynamic_index_in_dim(products, 1 - core, 0, keepdims=False)
    product = (
        own.astype(jnp.float32) + swap_cores(partner).astype(jnp.float32)
    ).astype(jnp.bfloat16)
    note = jnp.stack([sample_owner, sample_slot], 1).astype(jnp.bfloat16)
    note = jnp.pad(note, ((0, slots - samples), (0, 126)))
    message = jnp.concatenate(
        [
            product.reshape(devices, slots, half),
            jnp.broadcast_to(note[None], (devices, *note.shape)),
        ],
        2,
    )
    spread = lax.all_to_all(message, DP, split_axis=0, concat_axis=0, tiled=True)
    asked = spread[:, :samples, half : half + 2].astype(jnp.int32)
    wanted = (asked[:, :, 0] * slots + asked[:, :, 1]).reshape(devices * samples)
    (chosen,) = stored(one_hot(wanted, devices * slots))
    picked = dot(chosen, spread[:, :, :half].reshape(devices * slots, half)).astype(jnp.bfloat16)

    tokens = tokens.reshape(samples, patches, width).transpose(1, 0, 2).reshape(tok_rows, width)
    (tokens,) = stored(tokens)
    normal_in, _ = normalize(tokens)
    (normed_in,) = stored(normal_in.astype(jnp.bfloat16))
    pre_act = dot(normed_in, fc_weight)
    inner = jnp.tanh(gelu_coef * (pre_act + 0.044715 * pre_act**3))
    slope = 0.5 * (1.0 + inner) + 0.5 * pre_act * (1.0 - inner * inner) * gelu_coef * (
        1.0 + 3.0 * 0.044715 * pre_act * pre_act
    )
    act_out, slope = stored((0.5 * pre_act * (1.0 + inner)).astype(jnp.bfloat16), slope)
    (mlp_part,) = stored(dot(act_out, proj_weight).astype(jnp.bfloat16))
    mlp_out = mlp_part.astype(jnp.float32) + swap_cores(mlp_part).astype(jnp.float32)
    hidden = tokens.astype(jnp.float32) + mlp_out
    normal_out, inverse = normalize(hidden)
    normal_out, normed_out, inverse = stored(normal_out, normal_out.astype(jnp.bfloat16), inverse)

    own_cols = jnp.where(core == 0, normed_out[:, :half], normed_out[:, half:])
    both = jnp.concatenate([picked, own_cols], 1).reshape(devices, samples, width)
    (both,) = stored(lax.all_to_all(both, DP, split_axis=0, concat_axis=0, tiled=True))
    both = both.reshape(tok_rows, width)
    asking = dot(chosen, both[:, half:], 0, 0).astype(jnp.bfloat16)
    asking = lax.all_to_all(
        asking.reshape(devices, slots, half), DP, split_axis=0, concat_axis=0, tiled=True
    ).reshape(devices * slots, half)

    (head_wide,) = stored(jnp.pad(head_weight, ((0, 0), (0, wide - feats))).T)
    (pred_scaled,) = stored((dot(normed_out, head_wide, 1, 1) * loss_scale).astype(jnp.bfloat16))
    (pred_part,) = stored(dot(pred_scaled, head_wide).astype(jnp.bfloat16))
    pred_norm = pred_part.astype(jnp.float32) + swap_cores(pred_part).astype(jnp.float32)
    source = row_source()
    (pick,) = stored(one_hot(source, width))
    (fc_left,) = stored(dot(pick, normed_in, 1, 1).astype(jnp.bfloat16))
    (head_left,) = stored(dot(pick, normed_out, 1, 1).astype(jnp.bfloat16))
    pred_norm, head_pred = stored(pred_norm, dot(head_left, pred_scaled))
    pick_own, pick_other = stored(
        one_hot(source - core * half, half), one_hot(source - (1 - core) * half, half)
    )

    mine = both[:, :half]
    (other,) = stored(swap_cores(mine))
    target_norm = jnp.concatenate(
        [jnp.where(core == 0, mine, other), jnp.where(core == 0, other, mine)], 1
    )
    grad_norm = pred_norm - target_norm.astype(jnp.float32)
    grad_hidden = inverse * (
        grad_norm
        - jnp.mean(grad_norm, axis=-1, keepdims=True)
        - normal_out * jnp.mean(grad_norm * normal_out, axis=-1, keepdims=True)
    )
    (grad_hidden,) = stored(grad_hidden.astype(jnp.bfloat16))
    (proj_left,) = stored(dot(pick, grad_hidden, 1, 1).astype(jnp.bfloat16))
    (proj_grad,) = stored(dot(proj_left, act_out).astype(jnp.bfloat16))
    (grad_pre,) = stored(
        (dot(grad_hidden, proj_weight, 1, 1) * slope).astype(jnp.bfloat16)
    )
    (fc_grad,) = stored(dot(fc_left, grad_pre).astype(jnp.bfloat16))
    fc_cut, proj_cut = 1280, 640
    streams = [
        first_halves(proj_grad[:, proj_cut:], ("y", "z", "x")),
        first_halves(proj_grad[:, :proj_cut], ("x", "y", "z")),
        first_halves(fc_grad[:, fc_cut:], ("x", "y", "z")),
        first_halves(fc_grad[:, :fc_cut], ("z", "x", "y")),
    ]
    streams = exchange(streams, 0)
    streams, _ = together(streams)
    streams = exchange(streams, 1)
    streams, (asking,) = together(streams, asking)

    (asking_other,) = stored(swap_cores(asking))
    asking_left = (dot(pick_own, asking, 1, 1) + dot(pick_other, asking_other, 1, 1)).astype(
        jnp.bfloat16
    )
    (asking_left,) = stored(asking_left)
    (head_grad,) = stored(
        (head_pred - loss_scale * dot(asking_left, teacher_rows)).astype(jnp.bfloat16)
    )
    head_streams = [
        first_halves(head_grad[:, :640], ("z", "x", "y")),
        first_halves(head_grad[:, 640:1152], ("x", "y", "z")),
        first_halves(head_grad[:, 1152:], ("y", "z", "x")),
    ]
    for turn in range(2, 6):
        streams = exchange(streams, turn)
        if turn < 5:
            streams, _ = together(streams)
    for turn in range(6):
        head_streams = exchange(head_streams, turn)
        if turn < 5:
            head_streams, _ = together(head_streams)
    fc_shard = jnp.concatenate([streams[3], streams[2]], 1)
    proj_shard = jnp.concatenate([streams[1], streams[0]], 1)
    head_shard = jnp.concatenate(head_streams, 1)[:, :feats]
    return (fc_shard, proj_shard.T, head_shard)


def solution(mesh):
    torus = Mesh(mesh.devices.reshape(SIDE, SIDE, SIDE, 2), (*DP, "mp"))
    in_specs = (
        P(DP, None),
        P(DP),
        P(DP),
        P(DP, None, "mp"),
        P(None, "mp"),
        P("mp", None),
        P(None, "mp"),
    )
    out_specs = (P(DP, "mp"), P("mp", DP), P(DP, "mp"))
    return jax.shard_map(
        per_device, mesh=torus, in_specs=in_specs, out_specs=out_specs, check_vma=False
    )
```

```python
import functools
import math

import jax
import jax.numpy as jnp
from jax import lax
from jax.experimental import pallas as pl
from jax.experimental.pallas import tpu as pltpu
from jax.sharding import Mesh, PartitionSpec as P

gelu_coef = 0.7978845608
DP = ("z", "x", "y")
SIDE = 4
RING = list(range(SIDE))
TILE = 16


def normalize(values):
    values = values.astype(jnp.float32)
    center = jnp.mean(values, axis=-1, keepdims=True)
    spread = jnp.mean((values - center) ** 2, axis=-1, keepdims=True)
    inverse = 1.0 / jnp.sqrt(spread + 1e-06)
    return ((values - center) * inverse, inverse)


def dot(a, b, ca=1, cb=0):
    return lax.dot_general(a, b, (((ca,), (cb,)), ((), ())), preferred_element_type=jnp.float32)


def stored(*values):
    return lax.optimization_barrier(values)


def swap_cores(part):
    return lax.ppermute(part, "mp", [(0, 1), (1, 0)])


def spread_kernel(scale, core_ref, block_ref, weight_ref, rows_ref, own_ref, other_ref):
    slots, patches, feats = block_ref.shape
    rows = slots * patches
    to = lax.broadcasted_iota(jnp.int32, (rows, rows), 0)
    source = lax.broadcasted_iota(jnp.int32, (rows, rows), 1)
    pick = (source == (to % slots) * patches + to // slots).astype(jnp.bfloat16)
    moved = dot(pick, block_ref[...].reshape(rows, feats)).astype(jnp.bfloat16)
    rows_ref[:, :feats] = moved
    rows_ref[:, feats:] = jnp.zeros((rows, rows_ref.shape[1] - feats), jnp.bfloat16)
    product = dot(moved, weight_ref[...]) * scale
    half = product.shape[1] // 2
    first = core_ref[0] == 0
    own_ref[...] = jnp.where(first, product[:, :half], product[:, half:]).astype(jnp.bfloat16)
    other_ref[...] = jnp.where(first, product[:, half:], product[:, :half]).astype(jnp.bfloat16)


def patch_major(core, teacher_cache, weight, scale, wide):
    slots, patches, feats = teacher_cache.shape
    width = weight.shape[1]
    part = pl.BlockSpec((TILE * slots, width // 2), lambda i: (i, 0))
    return pl.pallas_call(
        functools.partial(spread_kernel, scale),
        grid=(patches // TILE,),
        in_specs=[
            pl.BlockSpec(memory_space=pltpu.SMEM),
            pl.BlockSpec((slots, TILE, feats), lambda i: (0, i, 0)),
            pl.BlockSpec((feats, width), lambda i: (0, 0)),
        ],
        out_specs=[pl.BlockSpec((TILE * slots, wide), lambda i: (i, 0)), part, part],
        out_shape=[
            jax.ShapeDtypeStruct((patches * slots, wide), jnp.bfloat16),
            jax.ShapeDtypeStruct((patches * slots, width // 2), jnp.bfloat16),
            jax.ShapeDtypeStruct((patches * slots, width // 2), jnp.bfloat16),
        ],
        compiler_params=pltpu.CompilerParams(vmem_limit_bytes=40 * 2**20),
    )(core, teacher_cache, weight)


def message_kernel(own_ref, came_ref, note_ref, out_ref):
    devices, slots, _ = out_ref.shape
    half = own_ref.shape[1]
    total = own_ref[...].astype(jnp.float32) + came_ref[...].astype(jnp.float32)
    out_ref[:, :, :half] = total.astype(jnp.bfloat16).reshape(devices, slots, half)
    note = note_ref[...]
    out_ref[:, :, half:] = jnp.broadcast_to(note[None], (devices, *note.shape))


def pick_kernel(core_ref, spread_ref, normed_ref, both_ref, asked_ref):
    devices, slots, across = spread_ref.shape
    tok_rows, width = normed_ref.shape
    half = width // 2
    samples = tok_rows // devices
    note = spread_ref[:, :, half:].astype(jnp.float32)[:, :samples, :].reshape(tok_rows, across - half)
    column = (note[:, 0:1] * slots + note[:, 1:2]).astype(jnp.int32)
    blocks = lax.broadcasted_iota(jnp.int32, (tok_rows, devices * slots), 1)
    chosen = (column == blocks).astype(jnp.bfloat16)
    rows = spread_ref[:, :, :half].reshape(devices * slots, half)
    both_ref[:, :half] = dot(chosen, rows).astype(jnp.bfloat16)
    normed = normed_ref[...]
    both_ref[:, half:] = jnp.where(core_ref[0] == 0, normed[:, :half], normed[:, half:])
    turned = note.T
    line = (turned[0:1, :] * slots + turned[1:2, :]).astype(jnp.int32)
    blocks = lax.broadcasted_iota(jnp.int32, (devices * slots, tok_rows), 0)
    asked_ref[...] = (line == blocks).astype(jnp.bfloat16)


def head_kernel(
    scale, own_ref, other_ref, pick_own_ref, pick_other_ref, rows_ref, left_ref, pred_ref, out_ref
):
    asking = dot(pick_own_ref[...], own_ref[...], 1, 1) + dot(
        pick_other_ref[...], other_ref[...], 1, 1
    )
    asking = asking.astype(jnp.bfloat16)
    wide = out_ref.shape[1]
    for start in range(0, wide, 512):
        cols = slice(start, min(start + 512, wide))
        out_ref[:, cols] = (
            dot(left_ref[...], pred_ref[:, cols]) - scale * dot(asking, rows_ref[:, cols])
        ).astype(jnp.bfloat16)


def whole(kernel, shapes, args, scalar=False):
    specs = [pl.BlockSpec(memory_space=pltpu.VMEM) for _ in args]
    if scalar:
        specs[0] = pl.BlockSpec(memory_space=pltpu.SMEM)
    outs = [jax.ShapeDtypeStruct(shape, jnp.bfloat16) for shape in shapes]
    return pl.pallas_call(
        kernel,
        in_specs=specs,
        out_specs=[pl.BlockSpec(memory_space=pltpu.VMEM) for _ in outs],
        out_shape=outs,
        compiler_params=pltpu.CompilerParams(vmem_limit_bytes=48 * 2**20),
    )(*args)


def first_mate(t, core):
    return t ^ 1 if core == 0 else 3 - t


def second_mate(t, core):
    return 3 - t if core == 0 else t ^ 1


def cubes(mate):
    groups = {}
    for core in (0, 1):
        for chip in range(SIDE**3):
            digits = (chip // SIDE**2, chip // SIDE % SIDE, chip % SIDE)
            sides = [sorted((t, mate(t, core))) for t in digits]
            group = tuple(
                ((z * SIDE + x) * SIDE + y) * 2 + core
                for z in sides[0]
                for x in sides[1]
                for y in sides[2]
            )
            groups[group] = True
    return [list(group) for group in groups]


def row_source(cube):
    rows = jnp.arange(SIDE**3 * TILE, dtype=jnp.int32)
    core = lax.axis_index("mp")
    source = rows % TILE
    for place, axis in enumerate(DP):
        step = SIDE ** (2 - place) * TILE
        t = lax.axis_index(axis)
        first = jnp.where(core == 0, t ^ 1, 3 - t)
        if cube:
            upper = rows // (2 ** (5 - place) * TILE) % 2
            lower = rows // (2 ** (2 - place) * TILE) % 2
            member = jnp.where(upper == 0, jnp.minimum(t, first), jnp.maximum(t, first))
        else:
            upper = rows // (2 * step) % 2
            lower = rows // step % 2
            member = jnp.where(upper == 0, first, t)
        second = jnp.where(core == 0, 3 - member, member ^ 1)
        digit = jnp.where(lower == 0, jnp.minimum(member, second), jnp.maximum(member, second))
        source = source + digit * step
    return source


def one_hot(source, size):
    return (source[:, None] == jnp.arange(size, dtype=jnp.int32)[None, :]).astype(jnp.bfloat16)


def halves(values, axis):
    dim = DP.index(axis)
    half = values.shape[dim] // 2
    return (
        lax.slice_in_dim(values, 0, half, axis=dim),
        lax.slice_in_dim(values, half, 2 * half, axis=dim),
    )


def exchange(streams, turn):
    pairs = [(p * 2 + c, first_mate(p, c) * 2 + c) for p in RING for c in (0, 1)]
    came = [lax.ppermute(sent, (order[turn], "mp"), pairs) for sent, _, order in streams]
    totals = [
        (kept.astype(jnp.float32) + part.astype(jnp.float32)).astype(jnp.bfloat16)
        for (_, kept, _), part in zip(streams, came)
    ]
    if turn == 2:
        return totals
    return [
        (*halves(total, order[turn + 1]), order) for total, (_, _, order) in zip(totals, streams)
    ]


def together(streams, *others):
    flat = stored(*(x for sent, kept, _ in streams for x in (sent, kept)), *others)
    count = 2 * len(streams)
    joined = [
        (flat[2 * i], flat[2 * i + 1], order) for i, (_, _, order) in enumerate(streams)
    ]
    return joined, flat[count:]


def cube_sum(pieces, groups):
    came = lax.all_to_all(
        pieces, (*DP, "mp"), split_axis=0, concat_axis=0, tiled=True, axis_index_groups=groups
    )
    total = came[0].astype(jnp.float32)
    for part in came[1:]:
        total = total + part.astype(jnp.float32)
    return total


def per_device(
    tokens, sample_owner, sample_slot, teacher_cache, fc_weight, proj_weight, head_weight
):
    tok_rows, width = tokens.shape
    slots, patches, feats = teacher_cache.shape
    hidden_units = fc_weight.shape[1]
    samples = tok_rows // patches
    devices = SIDE**3
    half = width // 2
    wide = -(-feats // 128) * 128
    loss_scale = 1.0 / math.sqrt(tok_rows * devices)
    core = lax.axis_index("mp")
    core_at = core.reshape(1).astype(jnp.int32)

    teacher_rows, own, other = patch_major(
        core_at, teacher_cache, head_weight.T, loss_scale, wide
    )
    teacher_rows, own, other = stored(teacher_rows, own, other)
    note = jnp.stack([sample_owner, sample_slot], 1).astype(jnp.bfloat16)
    note = jnp.pad(note, ((0, slots - samples), (0, 126)))
    (message,) = whole(
        message_kernel, [(devices, slots, half + 128)], [own, swap_cores(other), note]
    )
    message, tokens = stored(message, tokens)
    spread = lax.all_to_all(message, DP, split_axis=0, concat_axis=0, tiled=True)

    tokens = tokens.reshape(samples, patches, width).transpose(1, 0, 2).reshape(tok_rows, width)
    (tokens,) = stored(tokens)
    normal_in, _ = normalize(tokens)
    (normed_in,) = stored(normal_in.astype(jnp.bfloat16))
    pre_act = dot(normed_in, fc_weight)
    inner = jnp.tanh(gelu_coef * (pre_act + 0.044715 * pre_act**3))
    slope = 0.5 * (1.0 + inner) + 0.5 * pre_act * (1.0 - inner * inner) * gelu_coef * (
        1.0 + 3.0 * 0.044715 * pre_act * pre_act
    )
    act_out, slope = stored((0.5 * pre_act * (1.0 + inner)).astype(jnp.bfloat16), slope)
    (mlp_part,) = stored(dot(act_out, proj_weight).astype(jnp.bfloat16))
    mlp_out = mlp_part.astype(jnp.float32) + swap_cores(mlp_part).astype(jnp.float32)
    hidden = tokens.astype(jnp.float32) + mlp_out
    normal_out, inverse = normalize(hidden)
    normal_out, normed_out, inverse = stored(normal_out, normal_out.astype(jnp.bfloat16), inverse)

    both, asked = whole(
        pick_kernel,
        [(tok_rows, width), (devices * slots, tok_rows)],
        [core_at, spread, normed_out],
        scalar=True,
    )
    both = lax.all_to_all(
        both.reshape(devices, samples, width), DP, split_axis=0, concat_axis=0, tiled=True
    )

    (head_wide,) = stored(jnp.pad(head_weight, ((0, 0), (0, wide - feats))).T)
    (pred_scaled,) = stored((dot(normed_out, head_wide, 1, 1) * loss_scale).astype(jnp.bfloat16))
    (pred_part,) = stored(dot(pred_scaled, head_wide).astype(jnp.bfloat16))
    pred_norm = pred_part.astype(jnp.float32) + swap_cores(pred_part).astype(jnp.float32)
    (pick,) = stored(one_hot(row_source(False), width))
    fc_left = dot(pick, normed_in, 1, 1).astype(jnp.bfloat16)
    source = row_source(True)
    head_left = dot(one_hot(source, width), normed_out, 1, 1).astype(jnp.bfloat16)
    pick_own = one_hot(source - core * half, half)
    pick_other = one_hot(source - (1 - core) * half, half)
    both, pred_norm, pick, fc_left, head_left, pick_own, pick_other = stored(
        both, pred_norm, pick, fc_left, head_left, pick_own, pick_other
    )

    both = both.reshape(tok_rows, width)
    mine = both[:, :half]
    asking = dot(asked, both[:, half:]).astype(jnp.bfloat16)
    mine, asking = stored(mine, asking)
    other = swap_cores(mine)
    target_norm = jnp.concatenate(
        [jnp.where(core == 0, mine, other), jnp.where(core == 0, other, mine)], 1
    )
    grad_norm = pred_norm - target_norm.astype(jnp.float32)
    grad_hidden = inverse * (
        grad_norm
        - jnp.mean(grad_norm, axis=-1, keepdims=True)
        - normal_out * jnp.mean(grad_norm * normal_out, axis=-1, keepdims=True)
    )
    (grad_hidden,) = stored(grad_hidden.astype(jnp.bfloat16))
    asking = lax.all_to_all(
        asking.reshape(devices, slots, half), DP, split_axis=0, concat_axis=0, tiled=True
    ).reshape(devices * slots, half)
    (proj_left,) = stored(dot(pick, grad_hidden, 1, 1).astype(jnp.bfloat16))
    (proj_grad,) = stored(dot(proj_left, act_out).astype(jnp.bfloat16))
    (grad_pre,) = stored(
        (dot(grad_hidden, proj_weight, 1, 1) * slope).astype(jnp.bfloat16)
    )
    (fc_grad,) = stored(dot(fc_left, grad_pre).astype(jnp.bfloat16))
    streams = []
    for grad, order in ((proj_grad, ("x", "y", "z")), (fc_grad, ("y", "z", "x"))):
        parts = grad.reshape(SIDE, SIDE, SIDE, TILE, hidden_units)
        streams.append((*halves(parts, order[0]), order))
    streams = exchange(streams, 0)

    (asking,) = stored(asking)
    (head_grad,) = whole(
        functools.partial(head_kernel, loss_scale),
        [(width, wide)],
        [asking, swap_cores(asking), pick_own, pick_other, teacher_rows, head_left, pred_scaled],
    )
    streams, (head_grad,) = together(streams, head_grad)
    head_sum = cube_sum(head_grad.reshape(8, 8 * TILE, wide), cubes(first_mate))
    streams = exchange(streams, 1)
    streams, _ = together(streams)
    proj_sum, fc_sum = exchange(streams, 2)
    sums = jnp.concatenate(
        [
            fc_sum.reshape(8, TILE, hidden_units),
            proj_sum.reshape(8, TILE, hidden_units),
            head_sum.astype(jnp.bfloat16).reshape(8, TILE, wide),
        ],
        2,
    )
    (sums,) = stored(sums)
    total = cube_sum(sums, cubes(second_mate))
    fc_shard = total[:, :hidden_units]
    proj_shard = total[:, hidden_units : 2 * hidden_units]
    head_shard = total[:, 2 * hidden_units : 2 * hidden_units + feats]
    return (fc_shard, proj_shard.T, head_shard)


def solution(mesh):
    torus = Mesh(mesh.devices.reshape(SIDE, SIDE, SIDE, 2), (*DP, "mp"))
    in_specs = (
        P(DP, None),
        P(DP),
        P(DP),
        P(DP, None, "mp"),
        P(None, "mp"),
        P("mp", None),
        P(None, "mp"),
    )
    out_specs = (P(DP, "mp"), P("mp", DP), P(DP, "mp"))
    return jax.shard_map(
        per_device, mesh=torus, in_specs=in_specs, out_specs=out_specs, check_vma=False
    )
```

```python
import functools
import math

import jax
import jax.numpy as jnp
from jax import lax
from jax.experimental import pallas as pl
from jax.experimental.pallas import tpu as pltpu
from jax.sharding import Mesh, PartitionSpec as P

gelu_coef = 0.7978845608
DP = ("z", "x", "y")
SIDE = 4
RING = list(range(SIDE))
TILE = 16


def normalize(values):
    values = values.astype(jnp.float32)
    center = jnp.mean(values, axis=-1, keepdims=True)
    spread = jnp.mean((values - center) ** 2, axis=-1, keepdims=True)
    inverse = 1.0 / jnp.sqrt(spread + 1e-06)
    return ((values - center) * inverse, inverse)


def dot(a, b, ca=1, cb=0):
    return lax.dot_general(a, b, (((ca,), (cb,)), ((), ())), preferred_element_type=jnp.float32)


def stored(*values):
    return lax.optimization_barrier(values)


def swap_cores(part):
    return lax.ppermute(part, "mp", [(0, 1), (1, 0)])


def spread_kernel(scale, core_ref, block_ref, weight_ref, rows_ref, own_ref, other_ref):
    slots, patches, feats = block_ref.shape
    rows = slots * patches
    to = lax.broadcasted_iota(jnp.int32, (rows, rows), 0)
    source = lax.broadcasted_iota(jnp.int32, (rows, rows), 1)
    pick = (source == (to % slots) * patches + to // slots).astype(jnp.bfloat16)
    moved = dot(pick, block_ref[...].reshape(rows, feats)).astype(jnp.bfloat16)
    rows_ref[:, :feats] = moved
    rows_ref[:, feats:] = jnp.zeros((rows, rows_ref.shape[1] - feats), jnp.bfloat16)
    product = dot(moved, weight_ref[...]) * scale
    half = product.shape[1] // 2
    first = core_ref[0] == 0
    own_ref[...] = jnp.where(first, product[:, :half], product[:, half:]).astype(jnp.bfloat16)
    other_ref[...] = jnp.where(first, product[:, half:], product[:, :half]).astype(jnp.bfloat16)


def patch_major(core, teacher_cache, weight, scale, wide):
    slots, patches, feats = teacher_cache.shape
    width = weight.shape[1]
    part = pl.BlockSpec((TILE * slots, width // 2), lambda i: (i, 0))
    return pl.pallas_call(
        functools.partial(spread_kernel, scale),
        grid=(patches // TILE,),
        in_specs=[
            pl.BlockSpec(memory_space=pltpu.SMEM),
            pl.BlockSpec((slots, TILE, feats), lambda i: (0, i, 0)),
            pl.BlockSpec((feats, width), lambda i: (0, 0)),
        ],
        out_specs=[pl.BlockSpec((TILE * slots, wide), lambda i: (i, 0)), part, part],
        out_shape=[
            jax.ShapeDtypeStruct((patches * slots, wide), jnp.bfloat16),
            jax.ShapeDtypeStruct((patches * slots, width // 2), jnp.bfloat16),
            jax.ShapeDtypeStruct((patches * slots, width // 2), jnp.bfloat16),
        ],
        compiler_params=pltpu.CompilerParams(vmem_limit_bytes=40 * 2**20),
    )(core, teacher_cache, weight)


def message_kernel(own_ref, came_ref, note_ref, out_ref):
    devices, slots, _ = out_ref.shape
    half = own_ref.shape[1]
    total = own_ref[...].astype(jnp.float32) + came_ref[...].astype(jnp.float32)
    out_ref[:, :, :half] = total.astype(jnp.bfloat16).reshape(devices, slots, half)
    note = note_ref[...]
    out_ref[:, :, half:] = jnp.broadcast_to(note[None], (devices, *note.shape))


def pick_kernel(core_ref, spread_ref, normed_ref, both_ref, asked_ref):
    devices, slots, across = spread_ref.shape
    tok_rows, width = normed_ref.shape
    half = width // 2
    samples = tok_rows // devices
    note = spread_ref[:, :, half:].astype(jnp.float32)[:, :samples, :].reshape(tok_rows, across - half)
    column = (note[:, 0:1] * slots + note[:, 1:2]).astype(jnp.int32)
    blocks = lax.broadcasted_iota(jnp.int32, (tok_rows, devices * slots), 1)
    chosen = (column == blocks).astype(jnp.bfloat16)
    rows = spread_ref[:, :, :half].reshape(devices * slots, half)
    both_ref[:, :half] = dot(chosen, rows).astype(jnp.bfloat16)
    normed = normed_ref[...]
    both_ref[:, half:] = jnp.where(core_ref[0] == 0, normed[:, :half], normed[:, half:])
    turned = note.T
    line = (turned[0:1, :] * slots + turned[1:2, :]).astype(jnp.int32)
    blocks = lax.broadcasted_iota(jnp.int32, (devices * slots, tok_rows), 0)
    asked_ref[...] = (line == blocks).astype(jnp.bfloat16)


def head_kernel(
    scale, own_ref, other_ref, pick_own_ref, pick_other_ref, rows_ref, left_ref, pred_ref, out_ref
):
    asking = dot(pick_own_ref[...], own_ref[...], 1, 1) + dot(
        pick_other_ref[...], other_ref[...], 1, 1
    )
    asking = asking.astype(jnp.bfloat16)
    wide = out_ref.shape[1]
    for start in range(0, wide, 512):
        cols = slice(start, min(start + 512, wide))
        out_ref[:, cols] = (
            dot(left_ref[...], pred_ref[:, cols]) - scale * dot(asking, rows_ref[:, cols])
        ).astype(jnp.bfloat16)


def mlp_kernel(tokens_ref, fc_ref, proj_ref, normed_ref, act_ref, slope_ref, part_ref, total_ref):
    step = pl.program_id(0)

    @pl.when(step == 0)
    def _():
        normal, _ = normalize(tokens_ref[...])
        normed_ref[...] = normal.astype(jnp.bfloat16)

    pre = dot(normed_ref[...], fc_ref[...])
    square = pre * pre
    inner = jnp.tanh(gelu_coef * (pre + 0.044715 * (square * pre)))
    act = (0.5 * pre * (1.0 + inner)).astype(jnp.bfloat16)
    act_ref[...] = act
    slope_ref[...] = 0.5 * (1.0 + inner) + 0.5 * pre * (1.0 - inner * inner) * gelu_coef * (
        1.0 + 3.0 * 0.044715 * square
    )
    term = dot(act, proj_ref[...])

    @pl.when(step == 0)
    def _():
        total_ref[...] = term

    @pl.when(step > 0)
    def _():
        total_ref[...] = total_ref[...] + term

    @pl.when(step == pl.num_programs(0) - 1)
    def _():
        part_ref[...] = total_ref[...].astype(jnp.bfloat16)


def mlp(tokens, fc_weight, proj_weight):
    rows, width = tokens.shape
    units = fc_weight.shape[1]
    block = 512
    full = pl.BlockSpec((rows, width), lambda i: (0, 0))
    cols = pl.BlockSpec((rows, block), lambda i: (0, i))
    return pl.pallas_call(
        mlp_kernel,
        grid=(units // block,),
        in_specs=[
            full,
            pl.BlockSpec((width, block), lambda i: (0, i)),
            pl.BlockSpec((block, width), lambda i: (i, 0)),
        ],
        out_specs=[full, cols, cols, full],
        out_shape=[
            jax.ShapeDtypeStruct((rows, width), jnp.bfloat16),
            jax.ShapeDtypeStruct((rows, units), jnp.bfloat16),
            jax.ShapeDtypeStruct((rows, units), jnp.float32),
            jax.ShapeDtypeStruct((rows, width), jnp.bfloat16),
        ],
        scratch_shapes=[pltpu.VMEM((rows, width), jnp.float32)],
        compiler_params=pltpu.CompilerParams(vmem_limit_bytes=40 * 2**20),
    )(tokens, fc_weight, proj_weight)


def head_out_kernel(
    scale, tokens_ref, part_ref, came_ref, weight_ref, normal_ref, normed_ref, inverse_ref, pred_ref, back_ref
):
    hidden = tokens_ref[...].astype(jnp.float32) + (
        part_ref[...].astype(jnp.float32) + came_ref[...].astype(jnp.float32)
    )
    normal, inverse = normalize(hidden)
    normed = normal.astype(jnp.bfloat16)
    normal_ref[...] = normal
    normed_ref[...] = normed
    inverse_ref[...] = inverse
    pred = (dot(normed, weight_ref[...], 1, 1) * scale).astype(jnp.bfloat16)
    feats = weight_ref.shape[0]
    pred_ref[:, :feats] = pred
    pred_ref[:, feats:] = jnp.zeros((pred.shape[0], pred_ref.shape[1] - feats), jnp.bfloat16)
    back_ref[...] = dot(pred, weight_ref[...]).astype(jnp.bfloat16)


def asked_kernel(both_ref, asked_ref, mine_ref, asking_ref):
    half = mine_ref.shape[1]
    mine_ref[...] = both_ref[:, :half]
    asking_ref[...] = dot(asked_ref[...], both_ref[:, half:]).astype(jnp.bfloat16)


def proj_kernel(
    core_ref, mine_ref, other_ref, back_ref, came_ref, normal_ref, inverse_ref, pick_ref, act_ref,
    hidden_ref, sent_ref, kept_ref,
):
    mine = mine_ref[...].astype(jnp.float32)
    other = other_ref[...].astype(jnp.float32)
    first = core_ref[0] == 0
    target = jnp.concatenate([jnp.where(first, mine, other), jnp.where(first, other, mine)], 1)
    grad = back_ref[...].astype(jnp.float32) + came_ref[...].astype(jnp.float32) - target
    normal = normal_ref[...]
    hidden = inverse_ref[...] * (
        grad
        - jnp.mean(grad, axis=-1, keepdims=True)
        - normal * jnp.mean(grad * normal, axis=-1, keepdims=True)
    )
    hidden = hidden.astype(jnp.bfloat16)
    hidden_ref[...] = hidden
    left = dot(pick_ref[...], hidden, 1, 1).astype(jnp.bfloat16)
    rows = sent_ref.shape[0]
    for start in range(0, sent_ref.shape[1], 512):
        cols = slice(start, start + 512)
        sent_ref[:, cols] = dot(left[:rows], act_ref[:, cols]).astype(jnp.bfloat16)
        kept_ref[:, cols] = dot(left[rows:], act_ref[:, cols]).astype(jnp.bfloat16)


def fc_kernel(hidden_ref, proj_ref, slope_ref, left_ref, sent_ref, kept_ref):
    grad = (dot(hidden_ref[...], proj_ref[...], 1, 1) * slope_ref[...]).astype(jnp.bfloat16)
    rows = sent_ref.shape[0]
    sent_ref[...] = dot(left_ref[:rows], grad).astype(jnp.bfloat16)
    kept_ref[...] = dot(left_ref[rows:], grad).astype(jnp.bfloat16)


def fc_product(grad_hidden, proj_weight, slope, left):
    rows, width = grad_hidden.shape
    units = proj_weight.shape[0]
    block = 512
    out = pl.BlockSpec((width // 2, block), lambda i: (0, i))
    shape = jax.ShapeDtypeStruct((width // 2, units), jnp.bfloat16)
    return pl.pallas_call(
        fc_kernel,
        grid=(units // block,),
        in_specs=[
            pl.BlockSpec((rows, width), lambda i: (0, 0)),
            pl.BlockSpec((block, width), lambda i: (i, 0)),
            pl.BlockSpec((rows, block), lambda i: (0, i)),
            pl.BlockSpec((width, rows), lambda i: (0, 0)),
        ],
        out_specs=[out, out],
        out_shape=[shape, shape],
        cost_estimate=cost(4 * rows * width * units),
        compiler_params=pltpu.CompilerParams(vmem_limit_bytes=40 * 2**20),
    )(grad_hidden, proj_weight, slope, left)


def added(left, right):
    return (left.astype(jnp.float32) + right.astype(jnp.float32)).astype(jnp.bfloat16)


def add_second_kernel(kept_ref, came_ref, sent_ref, next_ref):
    sent_ref[...] = added(kept_ref[:, :2], came_ref[:, :2])
    next_ref[...] = added(kept_ref[:, 2:], came_ref[:, 2:])


def add_third_kernel(kept_ref, came_ref, sent_ref, next_ref):
    sent_ref[...] = added(kept_ref[:, :, :2], came_ref[:, :, :2])
    next_ref[...] = added(kept_ref[:, :, 2:], came_ref[:, :, 2:])


def gather_kernel(orders, *refs):
    *ins, head_ref, out_ref = refs
    for z in (0, 1):
        for x in (0, 1):
            for y in (0, 1):
                at = {"z": z, "x": x, "y": y}
                piece = (z * 2 + x) * 2 + y
                start = 0
                for i, order in enumerate(orders):
                    a, b, c = (at[axis] for axis in order)
                    kept_ref, came_ref = ins[2 * i], ins[2 * i + 1]
                    cols = slice(start, start + kept_ref.shape[-1])
                    out_ref[piece, :, cols] = added(kept_ref[a, b, c], came_ref[a, b, c])
                    start = cols.stop
                rows = slice(piece * TILE, (piece + 1) * TILE)
                total = head_ref[0, rows].astype(jnp.float32)
                for member in range(1, 8):
                    total = total + head_ref[member, rows].astype(jnp.float32)
                out_ref[piece, :, start:] = total.astype(jnp.bfloat16)


def sum_kernel(came_ref, *out_refs):
    start = 0
    for out_ref in out_refs:
        cols = slice(start, start + out_ref.shape[1])
        total = came_ref[0, :, cols].astype(jnp.float32)
        for member in range(1, 8):
            total = total + came_ref[member, :, cols].astype(jnp.float32)
        out_ref[...] = total
        start = cols.stop


def cost(flops):
    return pl.CostEstimate(flops=flops, bytes_accessed=flops // 300, transcendentals=0)


def whole(kernel, shapes, args, scalar=False, kinds=None, flops=None):
    specs = [pl.BlockSpec(memory_space=pltpu.VMEM) for _ in args]
    if scalar:
        specs[0] = pl.BlockSpec(memory_space=pltpu.SMEM)
    kinds = kinds or [jnp.bfloat16] * len(shapes)
    outs = [jax.ShapeDtypeStruct(shape, kind) for shape, kind in zip(shapes, kinds)]
    return pl.pallas_call(
        kernel,
        in_specs=specs,
        out_specs=[pl.BlockSpec(memory_space=pltpu.VMEM) for _ in outs],
        out_shape=outs,
        cost_estimate=cost(flops) if flops else None,
        compiler_params=pltpu.CompilerParams(vmem_limit_bytes=48 * 2**20),
    )(*args)


def first_mate(t, core):
    return t ^ 1 if core == 0 else 3 - t


def second_mate(t, core):
    return 3 - t if core == 0 else t ^ 1


def cubes(mate):
    groups = {}
    for core in (0, 1):
        for chip in range(SIDE**3):
            digits = (chip // SIDE**2, chip // SIDE % SIDE, chip % SIDE)
            sides = [sorted((t, mate(t, core))) for t in digits]
            group = tuple(
                ((z * SIDE + x) * SIDE + y) * 2 + core
                for z in sides[0]
                for x in sides[1]
                for y in sides[2]
            )
            groups[group] = True
    return [list(group) for group in groups]


def row_source(order, cube):
    rows = jnp.arange(SIDE**3 * TILE, dtype=jnp.int32)
    core = lax.axis_index("mp")
    source = rows % TILE
    for place, axis in enumerate(order):
        step = SIDE ** (2 - place) * TILE
        t = lax.axis_index(axis)
        first = jnp.where(core == 0, t ^ 1, 3 - t)
        if cube:
            upper = rows // (2 ** (5 - place) * TILE) % 2
            lower = rows // (2 ** (2 - place) * TILE) % 2
            member = jnp.where(upper == 0, jnp.minimum(t, first), jnp.maximum(t, first))
        else:
            upper = rows // (2 * step) % 2
            lower = rows // step % 2
            member = jnp.where(upper == 0, first, t)
        second = jnp.where(core == 0, 3 - member, member ^ 1)
        digit = jnp.where(lower == 0, jnp.minimum(member, second), jnp.maximum(member, second))
        source = source + digit * (SIDE ** (2 - DP.index(axis)) * TILE)
    return source


def one_hot(source, size):
    return (source[:, None] == jnp.arange(size, dtype=jnp.int32)[None, :]).astype(jnp.bfloat16)


def swap_first(sent, axis):
    pairs = [(p * 2 + c, first_mate(p, c) * 2 + c) for p in RING for c in (0, 1)]
    return lax.ppermute(sent, (axis, "mp"), pairs)


def over_cube(pieces, mate):
    return lax.all_to_all(
        pieces, (*DP, "mp"), split_axis=0, concat_axis=0, tiled=True, axis_index_groups=cubes(mate)
    )


def per_device(
    tokens, sample_owner, sample_slot, teacher_cache, fc_weight, proj_weight, head_weight
):
    tok_rows, width = tokens.shape
    slots, patches, feats = teacher_cache.shape
    units = fc_weight.shape[1]
    samples = tok_rows // patches
    devices = SIDE**3
    half = width // 2
    wide = -(-feats // 128) * 128
    loss_scale = 1.0 / math.sqrt(tok_rows * devices)
    core = lax.axis_index("mp")
    core_at = core.reshape(1).astype(jnp.int32)

    teacher_rows, own, other = patch_major(
        core_at, teacher_cache, head_weight.T, loss_scale, wide
    )
    note = jnp.stack([sample_owner, sample_slot], 1).astype(jnp.bfloat16)
    note = jnp.pad(note, ((0, slots - samples), (0, 126)))
    (message,) = whole(
        message_kernel, [(devices, slots, half + 128)], [own, swap_cores(other), note]
    )
    message, tokens = stored(message, tokens)
    spread = lax.all_to_all(message, DP, split_axis=0, concat_axis=0, tiled=True)

    tokens = tokens.reshape(samples, patches, width).transpose(1, 0, 2).reshape(tok_rows, width)
    (tokens,) = stored(tokens)
    normed_in, act_out, slope, mlp_part = mlp(tokens, fc_weight, proj_weight)
    normal_out, normed_out, inverse, pred_scaled, back = whole(
        functools.partial(head_out_kernel, loss_scale),
        [(tok_rows, width), (tok_rows, width), (tok_rows, 1), (tok_rows, wide), (tok_rows, width)],
        [tokens, mlp_part, swap_cores(mlp_part), head_weight.T],
        kinds=[jnp.float32, jnp.bfloat16, jnp.float32, jnp.bfloat16, jnp.bfloat16],
    )

    both, asked = whole(
        pick_kernel,
        [(tok_rows, width), (devices * slots, tok_rows)],
        [core_at, spread, normed_out],
        scalar=True,
    )
    both = lax.all_to_all(
        both.reshape(devices, samples, width), DP, split_axis=0, concat_axis=0, tiled=True
    )

    proj_order, fc_order = ("x", "y", "z"), ("y", "z", "x")
    back_came = swap_cores(back)
    pick = one_hot(row_source(proj_order, False), width)
    fc_left = dot(one_hot(row_source(fc_order, False), width), normed_in, 1, 1).astype(jnp.bfloat16)
    source = row_source(DP, True)
    head_left = dot(one_hot(source, width), normed_out, 1, 1).astype(jnp.bfloat16)
    pick_own = one_hot(source - core * half, half)
    pick_other = one_hot(source - (1 - core) * half, half)
    both, back_came, pick, fc_left, head_left, pick_own, pick_other = stored(
        both, back_came, pick, fc_left, head_left, pick_own, pick_other
    )

    mine, asking = whole(
        asked_kernel,
        [(tok_rows, half), (devices * slots, half)],
        [both.reshape(tok_rows, width), asked],
    )
    grad_hidden, *proj_halves = whole(
        proj_kernel,
        [(tok_rows, width), (half, units), (half, units)],
        [
            core_at, mine, swap_cores(mine), back, back_came, normal_out, inverse, pick, act_out
        ],
        scalar=True,
        flops=2 * tok_rows * width * (width + units),
    )
    asking = lax.all_to_all(
        asking.reshape(devices, slots, half), DP, split_axis=0, concat_axis=0, tiled=True
    ).reshape(devices * slots, half)
    fc_halves = list(fc_product(grad_hidden, proj_weight, slope, fc_left))
    proj_came = swap_first(proj_halves[0], proj_order[0])
    fc_came = swap_first(fc_halves[0], fc_order[0])
    asking, proj_came, fc_came = stored(asking, proj_came, fc_came)
    (head_grad,) = whole(
        functools.partial(head_kernel, loss_scale),
        [(width, wide)],
        [asking, swap_cores(asking), pick_own, pick_other, teacher_rows, head_left, pred_scaled],
        flops=2 * width * (width * width + wide * (width + tok_rows)),
    )
    head_parts = over_cube(head_grad.reshape(8, 8 * TILE, wide), first_mate)

    streams = []
    for kept, came, order in (
        (fc_halves[1], fc_came, fc_order),
        (proj_halves[1], proj_came, proj_order),
    ):
        shape = (2, SIDE, SIDE, TILE, units)
        sent, kept = whole(
            add_second_kernel,
            [(2, 2, SIDE, TILE, units)] * 2,
            [kept.reshape(shape), came.reshape(shape)],
        )
        came = swap_first(sent, order[1])
        sent, kept = whole(add_third_kernel, [(2, 2, 2, TILE, units)] * 2, [kept, came])
        streams += [kept, swap_first(sent, order[2])]
    (pieces,) = whole(
        functools.partial(gather_kernel, (fc_order, proj_order)),
        [(8, TILE, 2 * units + wide)],
        [*streams, head_parts],
    )
    fc_shard, proj_shard, head_shard = whole(
        sum_kernel,
        [(TILE, units), (TILE, units), (TILE, wide)],
        [over_cube(pieces, second_mate)],
        kinds=[jnp.float32] * 3,
    )
    return (fc_shard, proj_shard.T, head_shard[:, :feats])


def solution(mesh):
    torus = Mesh(mesh.devices.reshape(SIDE, SIDE, SIDE, 2), (*DP, "mp"))
    in_specs = (
        P(DP, None),
        P(DP),
        P(DP),
        P(DP, None, "mp"),
        P(None, "mp"),
        P("mp", None),
        P(None, "mp"),
    )
    out_specs = (P(DP, "mp"), P("mp", DP), P(DP, "mp"))
    return jax.shard_map(
        per_device, mesh=torus, in_specs=in_specs, out_specs=out_specs, check_vma=False
    )
```

```python
import math

import jax
import jax.numpy as jnp
from jax import lax
from jax.experimental import pallas as pl
from jax.experimental.pallas import tpu as pltpu
from jax.sharding import Mesh, PartitionSpec as P

gelu_coef = 0.7978845608
DP = ("z", "x", "y")
SIDE = 4
RING = list(range(SIDE))
TILE = 16


def normalize(values):
    values = values.astype(jnp.float32)
    center = jnp.mean(values, axis=-1, keepdims=True)
    spread = jnp.mean((values - center) ** 2, axis=-1, keepdims=True)
    inverse = 1.0 / jnp.sqrt(spread + 1e-06)
    return ((values - center) * inverse, inverse)


def dot(a, b, ca=1, cb=0):
    return lax.dot_general(a, b, (((ca,), (cb,)), ((), ())), preferred_element_type=jnp.float32)


def stored(*values):
    return lax.optimization_barrier(values)


def swap_cores(part):
    return lax.ppermute(part, "mp", [(0, 1), (1, 0)])


def spread_kernel(block_ref, note_ref, out_ref):
    slots, patches, feats = block_ref.shape
    rows = slots * patches
    to = lax.broadcasted_iota(jnp.int32, (rows, rows), 0)
    source = lax.broadcasted_iota(jnp.int32, (rows, rows), 1)
    pick = (source == (to % slots) * patches + to // slots).astype(jnp.bfloat16)
    moved = dot(pick, block_ref[...].reshape(rows, feats)).astype(jnp.bfloat16)
    out_ref[:, :, :feats] = moved.reshape(patches, slots, feats)
    note = note_ref[...]
    out_ref[:, :, feats:] = jnp.broadcast_to(note[None], (patches, *note.shape))


def to_patch_major(teacher_cache, note):
    slots, patches, feats = teacher_cache.shape
    wide = feats + note.shape[1]
    return pl.pallas_call(
        spread_kernel,
        grid=(patches // TILE,),
        in_specs=[
            pl.BlockSpec((slots, TILE, feats), lambda i: (0, i, 0)),
            pl.BlockSpec(note.shape, lambda i: (0, 0)),
        ],
        out_specs=pl.BlockSpec((TILE, slots, wide), lambda i: (i, 0, 0)),
        out_shape=jax.ShapeDtypeStruct((patches, slots, wide), jnp.bfloat16),
        compiler_params=pltpu.CompilerParams(vmem_limit_bytes=32 * 2**20),
    )(teacher_cache, note)


def pick_kernel(spread_ref, out_ref):
    devices, slots, wide = spread_ref.shape
    tok_rows = out_ref.shape[0]
    samples = tok_rows // devices
    note = spread_ref[:, :, wide - 128 :].astype(jnp.float32)[:, :samples, :].reshape(tok_rows, 128)
    column = (note[:, 64:65] * slots + note[:, 65:66]).astype(jnp.int32)
    blocks = lax.broadcasted_iota(jnp.int32, (tok_rows, devices * slots), 1)
    chosen = (column == blocks).astype(jnp.bfloat16)
    for start in range(0, wide, 512):
        cols = slice(start, min(start + 512, wide))
        rows = spread_ref[:, :, cols].reshape(devices * slots, cols.stop - start)
        out_ref[:, cols] = dot(chosen, rows).astype(jnp.bfloat16)


def sum_kernel(came_ref, *out_refs):
    start = 0
    for out_ref in out_refs:
        cols = slice(start, start + out_ref.shape[1])
        total = came_ref[0, :, cols].astype(jnp.float32)
        for member in range(1, 8):
            total = total + came_ref[member, :, cols].astype(jnp.float32)
        out_ref[...] = total
        start = cols.stop


def whole(kernel, shapes, kind, *args):
    return pl.pallas_call(
        kernel,
        in_specs=[pl.BlockSpec(memory_space=pltpu.VMEM) for _ in args],
        out_specs=[pl.BlockSpec(memory_space=pltpu.VMEM) for _ in shapes],
        out_shape=[jax.ShapeDtypeStruct(shape, kind) for shape in shapes],
        compiler_params=pltpu.CompilerParams(vmem_limit_bytes=32 * 2**20),
    )(*args)


def first_mate(t, core):
    return t ^ 1 if core == 0 else 3 - t


def second_mate(t, core):
    return 3 - t if core == 0 else t ^ 1


def cubes(mate):
    groups = {}
    for core in (0, 1):
        for chip in range(SIDE**3):
            digits = (chip // SIDE**2, chip // SIDE % SIDE, chip % SIDE)
            sides = [sorted((t, mate(t, core))) for t in digits]
            group = tuple(
                ((z * SIDE + x) * SIDE + y) * 2 + core
                for z in sides[0]
                for x in sides[1]
                for y in sides[2]
            )
            groups[group] = True
    return [list(group) for group in groups]


def row_source(order):
    rows = jnp.arange(SIDE**3 * TILE, dtype=jnp.int32)
    core = lax.axis_index("mp")
    source = rows % TILE
    for place, axis in enumerate(order):
        inner = 2 - DP.index(axis)
        t = lax.axis_index(axis)
        first = jnp.where(core == 0, t ^ 1, 3 - t)
        member = jnp.where(rows // (2 ** (5 - place) * TILE) % 2 == 0, first, t)
        second = jnp.where(core == 0, 3 - member, member ^ 1)
        digit = jnp.where(
            rows // (2**inner * TILE) % 2 == 0,
            jnp.minimum(member, second),
            jnp.maximum(member, second),
        )
        source = source + digit * (SIDE**inner * TILE)
    return source


def arranger(order):
    source = row_source(order)
    picks = (source[:, None] == jnp.arange(source.shape[0], dtype=jnp.int32)[None, :]).astype(
        jnp.bfloat16
    )
    half = source.shape[0] // 2
    return picks[:half], picks[half:]


def swap_first(sent, axis):
    pairs = [(p * 2 + c, first_mate(p, c) * 2 + c) for p in RING for c in (0, 1)]
    return lax.ppermute(sent, (axis, "mp"), pairs)


def added(left, right):
    return (left.astype(jnp.float32) + right.astype(jnp.float32)).astype(jnp.bfloat16)


def scatter_sums(streams):
    orders = [order for _, _, order in streams]
    sents = [sent for sent, _, _ in streams]
    kepts = [kept for _, kept, _ in streams]
    for turn in range(3):
        cames = stored(*(swap_first(sent, order[turn]) for sent, order in zip(sents, orders)))
        if turn == 2:
            break
        half = kepts[0].shape[0] // 2
        sents = [added(kept[:half], came[:half]) for kept, came in zip(kepts, cames)]
        kepts = [added(kept[half:], came[half:]) for kept, came in zip(kepts, cames)]
    pieces = jnp.concatenate(
        [added(kept, came).reshape(8, TILE, -1) for kept, came in zip(kepts, cames)], 2
    )
    (pieces,) = stored(pieces)
    came = lax.all_to_all(
        pieces,
        (*DP, "mp"),
        split_axis=0,
        concat_axis=0,
        tiled=True,
        axis_index_groups=cubes(second_mate),
    )
    return whole(sum_kernel, [(TILE, kept.shape[1]) for kept in kepts], jnp.float32, came)


def per_device(
    tokens, sample_owner, sample_slot, teacher_cache, fc_weight, proj_weight, head_weight
):
    tok_rows, width = tokens.shape
    slots, patches, feats = teacher_cache.shape
    samples = tok_rows // patches
    devices = SIDE**3
    wide = -(-feats // 128) * 128
    loss_scale = 1.0 / math.sqrt(tok_rows * devices)
    note = jnp.stack([sample_owner, sample_slot], 1).astype(jnp.bfloat16)
    note = jnp.pad(note, ((0, slots - samples), (0, wide - feats - 2)))
    spread = lax.all_to_all(
        to_patch_major(teacher_cache, note), DP, split_axis=0, concat_axis=0, tiled=True
    )
    (rows_out,) = whole(pick_kernel, [(devices * samples, wide)], jnp.bfloat16, spread)
    target = lax.all_to_all(
        rows_out.reshape(devices, samples, wide), DP, split_axis=0, concat_axis=0, tiled=True
    ).reshape(tok_rows, wide)

    tokens = tokens.reshape(samples, patches, width).transpose(1, 0, 2).reshape(tok_rows, width)
    (tokens,) = stored(tokens)
    normal_in, _ = normalize(tokens)
    (normed_in,) = stored(normal_in.astype(jnp.bfloat16))
    pre_act = dot(normed_in, fc_weight)
    inner = jnp.tanh(gelu_coef * (pre_act + 0.044715 * pre_act**3))
    slope = 0.5 * (1.0 + inner) + 0.5 * pre_act * (1.0 - inner * inner) * gelu_coef * (
        1.0 + 3.0 * 0.044715 * pre_act * pre_act
    )
    act_out, slope = stored((0.5 * pre_act * (1.0 + inner)).astype(jnp.bfloat16), slope)
    (mlp_part,) = stored(dot(act_out, proj_weight).astype(jnp.bfloat16))
    mlp_out = mlp_part.astype(jnp.float32) + swap_cores(mlp_part).astype(jnp.float32)
    hidden = tokens.astype(jnp.float32) + mlp_out
    normal_out, inverse = normalize(hidden)
    normal_out, normed_out, inverse = stored(normal_out, normal_out.astype(jnp.bfloat16), inverse)
    head_wide = jnp.pad(head_weight, ((0, 0), (0, wide - feats)))
    (head_wide,) = stored(head_wide.T)
    (pred,) = stored(dot(normed_out, head_wide, 1, 1))

    orders = {"head": ("z", "x", "y"), "proj": ("x", "y", "z"), "fc": ("y", "z", "x")}
    picks = {name: stored(*arranger(order)) for name, order in orders.items()}

    def turned(name, values):
        return stored(*(dot(pick, values, 1, 1).astype(jnp.bfloat16) for pick in picks[name]))

    head_left = turned("head", normed_out)
    fc_left = turned("fc", normed_in)

    (err_scaled,) = stored(
        ((pred - target.astype(jnp.float32)) * loss_scale).astype(jnp.bfloat16)
    )
    (grad_part,) = stored(dot(err_scaled, head_wide).astype(jnp.bfloat16))
    head_sent, head_kept = (dot(left, err_scaled).astype(jnp.bfloat16) for left in head_left)
    grad_came, head_sent, head_kept = stored(swap_cores(grad_part), head_sent, head_kept)
    grad_norm = grad_part.astype(jnp.float32) + grad_came.astype(jnp.float32)
    grad_hidden = inverse * (
        grad_norm
        - jnp.mean(grad_norm, axis=-1, keepdims=True)
        - normal_out * jnp.mean(grad_norm * normal_out, axis=-1, keepdims=True)
    )
    (grad_hidden,) = stored(grad_hidden.astype(jnp.bfloat16))
    proj_left = turned("proj", grad_hidden)
    proj_halves = stored(*(dot(left, act_out).astype(jnp.bfloat16) for left in proj_left))
    (grad_pre,) = stored(
        (dot(grad_hidden, proj_weight, 1, 1) * slope).astype(jnp.bfloat16)
    )
    fc_halves = stored(*(dot(left, grad_pre).astype(jnp.bfloat16) for left in fc_left))
    fc_shard, proj_shard, head_shard = scatter_sums(
        [
            (*fc_halves, orders["fc"]),
            (*proj_halves, orders["proj"]),
            (head_sent, head_kept, orders["head"]),
        ]
    )
    return (fc_shard, proj_shard.T, head_shard[:, :feats])


def solution(mesh):
    torus = Mesh(mesh.devices.reshape(SIDE, SIDE, SIDE, 2), (*DP, "mp"))
    in_specs = (
        P(DP, None),
        P(DP),
        P(DP),
        P(DP, None, "mp"),
        P(None, "mp"),
        P("mp", None),
        P(None, "mp"),
    )
    out_specs = (P(DP, "mp"), P("mp", DP), P(DP, "mp"))
    return jax.shard_map(
        per_device, mesh=torus, in_specs=in_specs, out_specs=out_specs, check_vma=False
    )
```

```python
import math

import jax
import jax.numpy as jnp
from jax import lax
from jax.experimental import pallas as pl
from jax.experimental.pallas import tpu as pltpu
from jax.sharding import Mesh, PartitionSpec as P

gelu_coef = 0.7978845608
DP = ("z", "x", "y")
SIDE = 4
RING = list(range(SIDE))
TILE = 16


def normalize(values):
    values = values.astype(jnp.float32)
    center = jnp.mean(values, axis=-1, keepdims=True)
    spread = jnp.mean((values - center) ** 2, axis=-1, keepdims=True)
    inverse = 1.0 / jnp.sqrt(spread + 1e-06)
    return ((values - center) * inverse, inverse)


def dot(a, b, ca=1, cb=0):
    return lax.dot_general(a, b, (((ca,), (cb,)), ((), ())), preferred_element_type=jnp.float32)


def stored(*values):
    return lax.optimization_barrier(values)


def swap_cores(part):
    return lax.ppermute(part, "mp", [(0, 1), (1, 0)])


def spread_kernel(block_ref, note_ref, out_ref):
    slots, patches, feats = block_ref.shape
    rows = slots * patches
    to = lax.broadcasted_iota(jnp.int32, (rows, rows), 0)
    source = lax.broadcasted_iota(jnp.int32, (rows, rows), 1)
    pick = (source == (to % slots) * patches + to // slots).astype(jnp.bfloat16)
    moved = dot(pick, block_ref[...].reshape(rows, feats)).astype(jnp.bfloat16)
    out_ref[:, :, :feats] = moved.reshape(patches, slots, feats)
    note = note_ref[...]
    out_ref[:, :, feats:] = jnp.broadcast_to(note[None], (patches, *note.shape))


def to_patch_major(teacher_cache, note):
    slots, patches, feats = teacher_cache.shape
    wide = feats + note.shape[1]
    return pl.pallas_call(
        spread_kernel,
        grid=(patches // TILE,),
        in_specs=[
            pl.BlockSpec((slots, TILE, feats), lambda i: (0, i, 0)),
            pl.BlockSpec(note.shape, lambda i: (0, 0)),
        ],
        out_specs=pl.BlockSpec((TILE, slots, wide), lambda i: (i, 0, 0)),
        out_shape=jax.ShapeDtypeStruct((patches, slots, wide), jnp.bfloat16),
        compiler_params=pltpu.CompilerParams(vmem_limit_bytes=60 * 2**20),
    )(teacher_cache, note)


def pick_kernel(spread_ref, out_ref):
    devices, slots, wide = spread_ref.shape
    tok_rows = out_ref.shape[0]
    samples = tok_rows // devices
    note = spread_ref[:, :, wide - 128 :].astype(jnp.float32)[:, :samples, :].reshape(tok_rows, 128)
    column = (note[:, 64:65] * slots + note[:, 65:66]).astype(jnp.int32)
    blocks = lax.broadcasted_iota(jnp.int32, (tok_rows, devices * slots), 1)
    chosen = (column == blocks).astype(jnp.bfloat16)
    for start in range(0, wide, 512):
        cols = slice(start, min(start + 512, wide))
        rows = spread_ref[:, :, cols].reshape(devices * slots, cols.stop - start)
        out_ref[:, cols] = dot(chosen, rows).astype(jnp.bfloat16)


def sum_kernel(came_ref, *out_refs):
    start = 0
    for out_ref in out_refs:
        cols = slice(start, start + out_ref.shape[1])
        total = came_ref[0, :, cols].astype(jnp.float32)
        for member in range(1, 8):
            total = total + came_ref[member, :, cols].astype(jnp.float32)
        out_ref[...] = total
        start = cols.stop


def whole(kernel, shapes, kind, *args):
    return pl.pallas_call(
        kernel,
        in_specs=[pl.BlockSpec(memory_space=pltpu.VMEM) for _ in args],
        out_specs=[pl.BlockSpec(memory_space=pltpu.VMEM) for _ in shapes],
        out_shape=[jax.ShapeDtypeStruct(shape, kind) for shape in shapes],
        compiler_params=pltpu.CompilerParams(vmem_limit_bytes=32 * 2**20),
    )(*args)


def first_mate(t, core):
    return t ^ 1 if core == 0 else 3 - t


def second_mate(t, core):
    return 3 - t if core == 0 else t ^ 1


def cubes(mate):
    groups = {}
    for core in (0, 1):
        for chip in range(SIDE**3):
            digits = (chip // SIDE**2, chip // SIDE % SIDE, chip % SIDE)
            sides = [sorted((t, mate(t, core))) for t in digits]
            group = tuple(
                ((z * SIDE + x) * SIDE + y) * 2 + core
                for z in sides[0]
                for x in sides[1]
                for y in sides[2]
            )
            groups[group] = True
    return [list(group) for group in groups]


def row_source(order):
    rows = jnp.arange(SIDE**3 * TILE, dtype=jnp.int32)
    core = lax.axis_index("mp")
    source = rows % TILE
    for place, axis in enumerate(order):
        inner = 2 - DP.index(axis)
        t = lax.axis_index(axis)
        first = jnp.where(core == 0, t ^ 1, 3 - t)
        member = jnp.where(rows // (2 ** (5 - place) * TILE) % 2 == 0, first, t)
        second = jnp.where(core == 0, 3 - member, member ^ 1)
        digit = jnp.where(
            rows // (2**inner * TILE) % 2 == 0,
            jnp.minimum(member, second),
            jnp.maximum(member, second),
        )
        source = source + digit * (SIDE**inner * TILE)
    return source


def arranger(order):
    source = row_source(order)
    picks = (source[:, None] == jnp.arange(source.shape[0], dtype=jnp.int32)[None, :]).astype(
        jnp.bfloat16
    )
    half = source.shape[0] // 2
    return picks[:half], picks[half:]


def swap_first(sent, axis):
    pairs = [(p * 2 + c, first_mate(p, c) * 2 + c) for p in RING for c in (0, 1)]
    return lax.ppermute(sent, (axis, "mp"), pairs)


def added(left, right):
    return (left.astype(jnp.float32) + right.astype(jnp.float32)).astype(jnp.bfloat16)


def scatter_sums(streams):
    orders = [order for _, _, order in streams]
    sents = [sent for sent, _, _ in streams]
    kepts = [kept for _, kept, _ in streams]
    for turn in range(3):
        cames = stored(*(swap_first(sent, order[turn]) for sent, order in zip(sents, orders)))
        if turn == 2:
            break
        half = kepts[0].shape[0] // 2
        sents = [added(kept[:half], came[:half]) for kept, came in zip(kepts, cames)]
        kepts = [added(kept[half:], came[half:]) for kept, came in zip(kepts, cames)]
    pieces = jnp.concatenate(
        [added(kept, came).reshape(8, TILE, -1) for kept, came in zip(kepts, cames)], 2
    )
    (pieces,) = stored(pieces)
    came = lax.all_to_all(
        pieces,
        (*DP, "mp"),
        split_axis=0,
        concat_axis=0,
        tiled=True,
        axis_index_groups=cubes(second_mate),
    )
    return whole(sum_kernel, [(TILE, kept.shape[1]) for kept in kepts], jnp.float32, came)


def per_device(
    tokens, sample_owner, sample_slot, teacher_cache, fc_weight, proj_weight, head_weight
):
    tok_rows, width = tokens.shape
    slots, patches, feats = teacher_cache.shape
    samples = tok_rows // patches
    devices = SIDE**3
    wide = -(-feats // 128) * 128
    loss_scale = 1.0 / math.sqrt(tok_rows * devices)
    rows = tokens.reshape(samples, patches, width).transpose(1, 0, 2)
    core = lax.axis_index("mp")
    part = jnp.where(core == 0, rows[:, :, : width // 2], rows[:, :, width // 2 :])
    part = lax.all_to_all(part, DP, split_axis=0, concat_axis=0, tiled=True)
    note = jnp.stack([sample_owner, sample_slot], 1).astype(jnp.bfloat16)
    note = jnp.pad(note, ((0, slots - samples), (0, wide - feats - 2)))
    part, message = stored(part, to_patch_major(teacher_cache, note))
    spread = lax.all_to_all(message, DP, split_axis=0, concat_axis=0, tiled=True)
    (target,) = whole(pick_kernel, [(devices * samples, wide)], jnp.bfloat16, spread)

    part = part.reshape(tok_rows, width // 2)
    other = swap_cores(part)
    tokens = jnp.concatenate(
        [jnp.where(core == 0, part, other), jnp.where(core == 0, other, part)], 1
    )
    (tokens,) = stored(tokens)
    normal_in, _ = normalize(tokens)
    (normed_in,) = stored(normal_in.astype(jnp.bfloat16))
    pre_act = dot(normed_in, fc_weight)
    inner = jnp.tanh(gelu_coef * (pre_act + 0.044715 * pre_act**3))
    slope = 0.5 * (1.0 + inner) + 0.5 * pre_act * (1.0 - inner * inner) * gelu_coef * (
        1.0 + 3.0 * 0.044715 * pre_act * pre_act
    )
    act_out, slope = stored((0.5 * pre_act * (1.0 + inner)).astype(jnp.bfloat16), slope)
    (mlp_part,) = stored(dot(act_out, proj_weight).astype(jnp.bfloat16))
    mlp_out = mlp_part.astype(jnp.float32) + swap_cores(mlp_part).astype(jnp.float32)
    hidden = tokens.astype(jnp.float32) + mlp_out
    normal_out, inverse = normalize(hidden)
    normal_out, normed_out, inverse = stored(normal_out, normal_out.astype(jnp.bfloat16), inverse)
    head_wide = jnp.pad(head_weight, ((0, 0), (0, wide - feats)))
    (head_wide,) = stored(head_wide.T)
    (pred,) = stored(dot(normed_out, head_wide, 1, 1))

    orders = {"head": ("z", "x", "y"), "proj": ("x", "y", "z"), "fc": ("y", "z", "x")}
    picks = {name: stored(*arranger(order)) for name, order in orders.items()}

    def turned(name, values):
        return stored(*(dot(pick, values, 1, 1).astype(jnp.bfloat16) for pick in picks[name]))

    head_left = turned("head", normed_out)
    fc_left = turned("fc", normed_in)

    (err_scaled,) = stored(
        ((pred - target.astype(jnp.float32)) * loss_scale).astype(jnp.bfloat16)
    )
    (grad_part,) = stored(dot(err_scaled, head_wide).astype(jnp.bfloat16))
    head_sent, head_kept = (dot(left, err_scaled).astype(jnp.bfloat16) for left in head_left)
    grad_came, head_sent = stored(swap_cores(grad_part), head_sent)
    (head_kept,) = stored(head_kept)
    grad_norm = grad_part.astype(jnp.float32) + grad_came.astype(jnp.float32)
    grad_hidden = inverse * (
        grad_norm
        - jnp.mean(grad_norm, axis=-1, keepdims=True)
        - normal_out * jnp.mean(grad_norm * normal_out, axis=-1, keepdims=True)
    )
    (grad_hidden,) = stored(grad_hidden.astype(jnp.bfloat16))
    proj_left = turned("proj", grad_hidden)
    proj_halves = [stored(dot(left, act_out).astype(jnp.bfloat16))[0] for left in proj_left]
    (grad_pre,) = stored(
        (dot(grad_hidden, proj_weight, 1, 1) * slope).astype(jnp.bfloat16)
    )
    fc_halves = [stored(dot(left, grad_pre).astype(jnp.bfloat16))[0] for left in fc_left]
    fc_shard, proj_shard, head_shard = scatter_sums(
        [
            (*fc_halves, orders["fc"]),
            (*proj_halves, orders["proj"]),
            (head_sent, head_kept, orders["head"]),
        ]
    )
    return (fc_shard, proj_shard.T, head_shard[:, :feats])


def solution(mesh):
    torus = Mesh(mesh.devices.reshape(SIDE, SIDE, SIDE, 2), (*DP, "mp"))
    in_specs = (
        P(DP, None),
        P(DP),
        P(DP),
        P(DP, None, "mp"),
        P(None, "mp"),
        P("mp", None),
        P(None, "mp"),
    )
    out_specs = (P(DP, "mp"), P("mp", DP), P(DP, "mp"))
    return jax.shard_map(
        per_device, mesh=torus, in_specs=in_specs, out_specs=out_specs, check_vma=False
    )
```

```python
import functools
import math

import jax
import jax.numpy as jnp
from jax import lax
from jax.experimental import pallas as pl
from jax.experimental.pallas import tpu as pltpu
from jax.sharding import Mesh, PartitionSpec as P

gelu_coef = 0.7978845608
DP = ("z", "x", "y")
SIDE = 4
RING = list(range(SIDE))
TILE = 16


def normalize(values):
    values = values.astype(jnp.float32)
    center = jnp.mean(values, axis=-1, keepdims=True)
    spread = jnp.mean((values - center) ** 2, axis=-1, keepdims=True)
    inverse = 1.0 / jnp.sqrt(spread + 1e-06)
    return ((values - center) * inverse, inverse)


def dot(a, b, ca=1, cb=0):
    return lax.dot_general(a, b, (((ca,), (cb,)), ((), ())), preferred_element_type=jnp.float32)


def stored(*values):
    return lax.optimization_barrier(values)


def swap_cores(part):
    return lax.ppermute(part, "mp", [(0, 1), (1, 0)])


def spread_kernel(block_ref, note_ref, out_ref):
    slots, patches, feats = block_ref.shape
    rows = slots * patches
    to = lax.broadcasted_iota(jnp.int32, (rows, rows), 0)
    source = lax.broadcasted_iota(jnp.int32, (rows, rows), 1)
    pick = (source == (to % slots) * patches + to // slots).astype(jnp.bfloat16)
    moved = dot(pick, block_ref[...].reshape(rows, feats)).astype(jnp.bfloat16)
    out_ref[:, :, :feats] = moved.reshape(patches, slots, feats)
    note = note_ref[...]
    out_ref[:, :, feats:] = jnp.broadcast_to(note[None], (patches, *note.shape))


def to_patch_major(teacher_cache, note):
    slots, patches, feats = teacher_cache.shape
    wide = feats + note.shape[1]
    return pl.pallas_call(
        spread_kernel,
        grid=(patches // TILE,),
        in_specs=[
            pl.BlockSpec((slots, TILE, feats), lambda i: (0, i, 0)),
            pl.BlockSpec(note.shape, lambda i: (0, 0)),
        ],
        out_specs=pl.BlockSpec((TILE, slots, wide), lambda i: (i, 0, 0)),
        out_shape=jax.ShapeDtypeStruct((patches, slots, wide), jnp.bfloat16),
        compiler_params=pltpu.CompilerParams(vmem_limit_bytes=60 * 2**20),
    )(teacher_cache, note)


def pick_kernel(spread_ref, out_ref):
    devices, slots, wide = spread_ref.shape
    tok_rows = out_ref.shape[0]
    samples = tok_rows // devices
    note = spread_ref[:, :, wide - 128 :].astype(jnp.float32)[:, :samples, :].reshape(tok_rows, 128)
    column = (note[:, 64:65] * slots + note[:, 65:66]).astype(jnp.int32)
    blocks = lax.broadcasted_iota(jnp.int32, (tok_rows, devices * slots), 1)
    chosen = (column == blocks).astype(jnp.bfloat16)
    for start in range(0, wide, 512):
        cols = slice(start, min(start + 512, wide))
        rows = spread_ref[:, :, cols].reshape(devices * slots, cols.stop - start)
        out_ref[:, cols] = dot(chosen, rows).astype(jnp.bfloat16)


def added(left, right):
    return (left.astype(jnp.float32) + right.astype(jnp.float32)).astype(jnp.bfloat16)


def join_kernel(count, *refs):
    ins, (sent_ref, kept_ref) = refs[: 2 * count], refs[2 * count :]
    half = sent_ref.shape[0]
    start = 0
    for i in range(count):
        kept, came = ins[i], ins[count + i]
        cols = slice(start, start + kept.shape[1])
        sent_ref[:, cols] = added(kept[:half], came[:half])
        kept_ref[:, cols] = added(kept[half:], came[half:])
        start = cols.stop


def sum_kernel(cuts, came_ref, *out_refs):
    start = 0
    for name, first, last in cuts:
        cols = slice(start, start + last - first)
        total = came_ref[0, :, cols].astype(jnp.float32)
        for member in range(1, 8):
            total = total + came_ref[member, :, cols].astype(jnp.float32)
        out_refs[name][:, first:last] = total
        start = cols.stop


def whole(kernel, shapes, kind, *args):
    return pl.pallas_call(
        kernel,
        in_specs=[pl.BlockSpec(memory_space=pltpu.VMEM) for _ in args],
        out_specs=[pl.BlockSpec(memory_space=pltpu.VMEM) for _ in shapes],
        out_shape=[jax.ShapeDtypeStruct(shape, kind) for shape in shapes],
        compiler_params=pltpu.CompilerParams(vmem_limit_bytes=24 * 2**20),
    )(*args)


def first_mate(t, core):
    return t ^ 1 if core == 0 else 3 - t


def second_mate(t, core):
    return 3 - t if core == 0 else t ^ 1


def cubes(mate):
    groups = {}
    for core in (0, 1):
        for chip in range(SIDE**3):
            digits = (chip // SIDE**2, chip // SIDE % SIDE, chip % SIDE)
            sides = [sorted((t, mate(t, core))) for t in digits]
            group = tuple(
                ((z * SIDE + x) * SIDE + y) * 2 + core
                for z in sides[0]
                for x in sides[1]
                for y in sides[2]
            )
            groups[group] = True
    return [list(group) for group in groups]


def row_source(order, core):
    rows = jnp.arange(SIDE**3 * TILE, dtype=jnp.int32)
    source = rows % TILE
    for place, axis in enumerate(order):
        inner = 2 - DP.index(axis)
        t = lax.axis_index(axis)
        first = jnp.where(core == 0, t ^ 1, 3 - t)
        member = jnp.where(rows // (2 ** (5 - place) * TILE) % 2 == 0, first, t)
        second = jnp.where(core == 0, 3 - member, member ^ 1)
        digit = jnp.where(
            rows // (2**inner * TILE) % 2 == 0,
            jnp.minimum(member, second),
            jnp.maximum(member, second),
        )
        source = source + digit * (SIDE**inner * TILE)
    return source


def arranger(order, core):
    source = row_source(order, core)
    picks = (source[:, None] == jnp.arange(source.shape[0], dtype=jnp.int32)[None, :]).astype(
        jnp.bfloat16
    )
    half = source.shape[0] // 2
    return picks[:half], picks[half:]


def swap_first(sent, axis):
    pairs = [(p * 2 + c, first_mate(p, c) * 2 + c) for p in RING for c in (0, 1)]
    return lax.ppermute(sent, (axis, "mp"), pairs)


def scatter_sums(streams, cuts, shapes):
    orders = [order for _, _, order in streams]
    sents, kepts = [], []
    for kept_parts, came_parts, _ in streams:
        rows = kept_parts[0].shape[0]
        cols = sum(part.shape[1] for part in kept_parts)
        sent, kept = whole(
            functools.partial(join_kernel, len(kept_parts)),
            [(rows // 2, cols)] * 2,
            jnp.bfloat16,
            *kept_parts,
            *came_parts,
        )
        sents.append(sent)
        kepts.append(kept)
    for turn in (1, 2):
        cames = stored(*(swap_first(sent, order[turn]) for sent, order in zip(sents, orders)))
        if turn == 2:
            break
        half = kepts[0].shape[0] // 2
        sents = [added(kept[:half], came[:half]) for kept, came in zip(kepts, cames)]
        kepts = [added(kept[half:], came[half:]) for kept, came in zip(kepts, cames)]
    pieces = jnp.concatenate(
        [added(kept, came).reshape(8, TILE, -1) for kept, came in zip(kepts, cames)], 2
    )
    (pieces,) = stored(pieces)
    came = lax.all_to_all(
        pieces,
        (*DP, "mp"),
        split_axis=0,
        concat_axis=0,
        tiled=True,
        axis_index_groups=cubes(second_mate),
    )
    return whole(functools.partial(sum_kernel, cuts), shapes, jnp.float32, came)


def per_device(
    tokens, sample_owner, sample_slot, teacher_cache, fc_weight, proj_weight, head_weight
):
    tok_rows, width = tokens.shape
    slots, patches, feats = teacher_cache.shape
    samples = tok_rows // patches
    devices = SIDE**3
    wide = -(-feats // 128) * 128
    loss_scale = 1.0 / math.sqrt(tok_rows * devices)
    rows = tokens.reshape(samples, patches, width).transpose(1, 0, 2)
    core = lax.axis_index("mp")
    part = jnp.where(core == 0, rows[:, :, : width // 2], rows[:, :, width // 2 :])
    part = lax.all_to_all(part, DP, split_axis=0, concat_axis=0, tiled=True)
    note = jnp.stack([sample_owner, sample_slot], 1).astype(jnp.bfloat16)
    note = jnp.pad(note, ((0, slots - samples), (0, wide - feats - 2)))
    part, message = stored(part, to_patch_major(teacher_cache, note))
    spread = lax.all_to_all(message, DP, split_axis=0, concat_axis=0, tiled=True)
    (target,) = whole(pick_kernel, [(devices * samples, wide)], jnp.bfloat16, spread)

    part = part.reshape(tok_rows, width // 2)
    other = swap_cores(part)
    tokens = jnp.concatenate(
        [jnp.where(core == 0, part, other), jnp.where(core == 0, other, part)], 1
    )
    tokens, core = stored(tokens, core)
    normal_in, _ = normalize(tokens)
    (normed_in,) = stored(normal_in.astype(jnp.bfloat16))
    pre_act = dot(normed_in, fc_weight)
    inner = jnp.tanh(gelu_coef * (pre_act + 0.044715 * pre_act**3))
    slope = 0.5 * (1.0 + inner) + 0.5 * pre_act * (1.0 - inner * inner) * gelu_coef * (
        1.0 + 3.0 * 0.044715 * pre_act * pre_act
    )
    act_out, slope = stored((0.5 * pre_act * (1.0 + inner)).astype(jnp.bfloat16), slope)
    (mlp_part,) = stored(dot(act_out, proj_weight).astype(jnp.bfloat16))
    mlp_out = mlp_part.astype(jnp.float32) + swap_cores(mlp_part).astype(jnp.float32)
    hidden = tokens.astype(jnp.float32) + mlp_out
    normal_out, inverse = normalize(hidden)
    normal_out, normed_out, inverse = stored(normal_out, normal_out.astype(jnp.bfloat16), inverse)
    head_wide = jnp.pad(head_weight, ((0, 0), (0, wide - feats)))
    (head_wide,) = stored(head_wide.T)
    (pred,) = stored(dot(normed_out, head_wide, 1, 1))

    orders = {"z": ("z", "x", "y"), "x": ("x", "y", "z"), "y": ("y", "z", "x")}
    picks = {axis: stored(*arranger(order, core)) for axis, order in orders.items()}
    head_cut, fc_cut, proj_cut = (640, 1152), 640, 640

    def turned(axes, half, values):
        return {
            axis: stored(dot(picks[axis][half], values, 1, 1).astype(jnp.bfloat16))[0]
            for axis in axes
        }

    def product(left, values):
        return dot(left, values).astype(jnp.bfloat16)

    head_left = [turned("zxy", half, normed_out) for half in (0, 1)]
    fc_left = [turned("zy", half, normed_in) for half in (0, 1)]

    (err_scaled,) = stored(
        ((pred - target.astype(jnp.float32)) * loss_scale).astype(jnp.bfloat16)
    )
    (grad_part,) = stored(dot(err_scaled, head_wide).astype(jnp.bfloat16))
    head_parts = {
        "z": err_scaled[:, : head_cut[0]],
        "x": err_scaled[:, head_cut[0] : head_cut[1]],
        "y": err_scaled[:, head_cut[1] :],
    }
    grad_came, *head_sents = stored(
        swap_cores(grad_part), *(product(head_left[0][axis], head_parts[axis]) for axis in "zxy")
    )
    head_came = {axis: swap_first(sent, axis) for axis, sent in zip("zxy", head_sents)}
    head_kept = {axis: product(head_left[1][axis], head_parts[axis]) for axis in "zxy"}
    grad_norm = grad_part.astype(jnp.float32) + grad_came.astype(jnp.float32)
    grad_hidden = inverse * (
        grad_norm
        - jnp.mean(grad_norm, axis=-1, keepdims=True)
        - normal_out * jnp.mean(grad_norm * normal_out, axis=-1, keepdims=True)
    )
    (grad_hidden,) = stored(grad_hidden.astype(jnp.bfloat16))
    (grad_pre,) = stored(
        (dot(grad_hidden, proj_weight, 1, 1) * slope).astype(jnp.bfloat16)
    )
    fc_parts = {"z": grad_pre[:, :fc_cut], "y": grad_pre[:, fc_cut:]}
    proj_parts = {"z": act_out[:, :proj_cut], "x": act_out[:, proj_cut:]}
    proj_left = turned("zx", 0, grad_hidden)
    sents = {
        ("fc", "y"): product(fc_left[0]["y"], fc_parts["y"]),
        ("fc", "z"): product(fc_left[0]["z"], fc_parts["z"]),
        ("proj", "x"): product(proj_left["x"], proj_parts["x"]),
        ("proj", "z"): product(proj_left["z"], proj_parts["z"]),
    }
    sents = {key: stored(sent)[0] for key, sent in sents.items()}
    came = {
        key: swap_first(sent, key[1])
        for key, sent in sents.items()
    }
    fc_kept = {axis: product(fc_left[1][axis], fc_parts[axis]) for axis in "zy"}
    proj_left = turned("zx", 1, grad_hidden)
    proj_kept = {axis: product(proj_left[axis], proj_parts[axis]) for axis in "zx"}
    *head_cames, first, second, third, fourth = stored(*head_came.values(), *came.values())
    head_came = dict(zip(head_came, head_cames))
    came = dict(zip(came, (first, second, third, fourth)))
    streams = [
        (
            [head_kept["z"], fc_kept["z"], proj_kept["z"]],
            [head_came["z"], came["fc", "z"], came["proj", "z"]],
            orders["z"],
        ),
        ([head_kept["x"], proj_kept["x"]], [head_came["x"], came["proj", "x"]], orders["x"]),
        ([head_kept["y"], fc_kept["y"]], [head_came["y"], came["fc", "y"]], orders["y"]),
    ]
    units = fc_weight.shape[1]
    cuts = [
        (2, 0, head_cut[0]),
        (0, 0, fc_cut),
        (1, 0, proj_cut),
        (2, *head_cut),
        (1, proj_cut, units),
        (2, head_cut[1], wide),
        (0, fc_cut, units),
    ]
    fc_shard, proj_shard, head_shard = scatter_sums(
        streams, cuts, [(TILE, units), (TILE, units), (TILE, wide)]
    )
    return (fc_shard, proj_shard.T, head_shard[:, :feats])


def solution(mesh):
    torus = Mesh(mesh.devices.reshape(SIDE, SIDE, SIDE, 2), (*DP, "mp"))
    in_specs = (
        P(DP, None),
        P(DP),
        P(DP),
        P(DP, None, "mp"),
        P(None, "mp"),
        P("mp", None),
        P(None, "mp"),
    )
    out_specs = (P(DP, "mp"), P("mp", DP), P(DP, "mp"))
    return jax.shard_map(
        per_device, mesh=torus, in_specs=in_specs, out_specs=out_specs, check_vma=False
    )
```

```python
import functools
import math

import jax
import jax.numpy as jnp
from jax import lax
from jax.experimental import pallas as pl
from jax.experimental.pallas import tpu as pltpu
from jax.sharding import Mesh, PartitionSpec as P

gelu_coef = 0.7978845608
DP = ("z", "x", "y")
SIDE = 4
RING = list(range(SIDE))
TILE = 16


def normalize(values):
    values = values.astype(jnp.float32)
    center = jnp.mean(values, axis=-1, keepdims=True)
    spread = jnp.mean((values - center) ** 2, axis=-1, keepdims=True)
    inverse = 1.0 / jnp.sqrt(spread + 1e-06)
    return ((values - center) * inverse, inverse)


def dot(a, b, ca=1, cb=0):
    return lax.dot_general(a, b, (((ca,), (cb,)), ((), ())), preferred_element_type=jnp.float32)


def stored(*values):
    return lax.optimization_barrier(values)


def swap_cores(part):
    return lax.ppermute(part, "mp", [(0, 1), (1, 0)])


def spread_kernel(block_ref, note_ref, out_ref):
    slots, patches, feats = block_ref.shape
    rows = slots * patches
    to = lax.broadcasted_iota(jnp.int32, (rows, rows), 0)
    source = lax.broadcasted_iota(jnp.int32, (rows, rows), 1)
    pick = (source == (to % slots) * patches + to // slots).astype(jnp.bfloat16)
    moved = dot(pick, block_ref[...].reshape(rows, feats)).astype(jnp.bfloat16)
    out_ref[:, :, :feats] = moved.reshape(patches, slots, feats)
    note = note_ref[...]
    out_ref[:, :, feats:] = jnp.broadcast_to(note[None], (patches, *note.shape))


def to_patch_major(teacher_cache, note):
    slots, patches, feats = teacher_cache.shape
    wide = feats + note.shape[1]
    return pl.pallas_call(
        spread_kernel,
        grid=(patches // TILE,),
        in_specs=[
            pl.BlockSpec((slots, TILE, feats), lambda i: (0, i, 0)),
            pl.BlockSpec(note.shape, lambda i: (0, 0)),
        ],
        out_specs=pl.BlockSpec((TILE, slots, wide), lambda i: (i, 0, 0)),
        out_shape=jax.ShapeDtypeStruct((patches, slots, wide), jnp.bfloat16),
        compiler_params=pltpu.CompilerParams(vmem_limit_bytes=60 * 2**20),
    )(teacher_cache, note)


def pick_kernel(spread_ref, out_ref):
    devices, slots, wide = spread_ref.shape
    tok_rows = out_ref.shape[0]
    samples = tok_rows // devices
    note = spread_ref[:, :, wide - 128 :].astype(jnp.float32)[:, :samples, :].reshape(tok_rows, 128)
    column = (note[:, 64:65] * slots + note[:, 65:66]).astype(jnp.int32)
    blocks = lax.broadcasted_iota(jnp.int32, (tok_rows, devices * slots), 1)
    chosen = (column == blocks).astype(jnp.bfloat16)
    for start in range(0, wide, 512):
        cols = slice(start, min(start + 512, wide))
        rows = spread_ref[:, :, cols].reshape(devices * slots, cols.stop - start)
        out_ref[:, cols] = dot(chosen, rows).astype(jnp.bfloat16)


def added(left, right):
    return (left.astype(jnp.float32) + right.astype(jnp.float32)).astype(jnp.bfloat16)


def join_kernel(count, *refs):
    ins, (sent_ref, kept_ref) = refs[: 2 * count], refs[2 * count :]
    half = sent_ref.shape[0]
    start = 0
    for i in range(count):
        kept, came = ins[i], ins[count + i]
        cols = slice(start, start + kept.shape[1])
        sent_ref[:, cols] = added(kept[:half], came[:half])
        kept_ref[:, cols] = added(kept[half:], came[half:])
        start = cols.stop


def sum_kernel(cuts, came_ref, *out_refs):
    start = 0
    for name, first, last in cuts:
        cols = slice(start, start + last - first)
        total = came_ref[0, :, cols].astype(jnp.float32)
        for member in range(1, 8):
            total = total + came_ref[member, :, cols].astype(jnp.float32)
        out_refs[name][:, first:last] = total
        start = cols.stop


def whole(kernel, shapes, kind, *args):
    return pl.pallas_call(
        kernel,
        in_specs=[pl.BlockSpec(memory_space=pltpu.VMEM) for _ in args],
        out_specs=[pl.BlockSpec(memory_space=pltpu.VMEM) for _ in shapes],
        out_shape=[jax.ShapeDtypeStruct(shape, kind) for shape in shapes],
        compiler_params=pltpu.CompilerParams(vmem_limit_bytes=24 * 2**20),
    )(*args)


def first_mate(t, core):
    return t ^ 1 if core == 0 else 3 - t


def second_mate(t, core):
    return 3 - t if core == 0 else t ^ 1


def cubes(mate):
    groups = {}
    for core in (0, 1):
        for chip in range(SIDE**3):
            digits = (chip // SIDE**2, chip // SIDE % SIDE, chip % SIDE)
            sides = [sorted((t, mate(t, core))) for t in digits]
            group = tuple(
                ((z * SIDE + x) * SIDE + y) * 2 + core
                for z in sides[0]
                for x in sides[1]
                for y in sides[2]
            )
            groups[group] = True
    return [list(group) for group in groups]


def row_source(order, core):
    rows = jnp.arange(SIDE**3 * TILE, dtype=jnp.int32)
    source = rows % TILE
    for place, axis in enumerate(order):
        inner = 2 - DP.index(axis)
        t = lax.axis_index(axis)
        first = jnp.where(core == 0, t ^ 1, 3 - t)
        member = jnp.where(rows // (2 ** (5 - place) * TILE) % 2 == 0, first, t)
        second = jnp.where(core == 0, 3 - member, member ^ 1)
        digit = jnp.where(
            rows // (2**inner * TILE) % 2 == 0,
            jnp.minimum(member, second),
            jnp.maximum(member, second),
        )
        source = source + digit * (SIDE**inner * TILE)
    return source


def arranger(order, core):
    source = row_source(order, core)
    picks = (source[:, None] == jnp.arange(source.shape[0], dtype=jnp.int32)[None, :]).astype(
        jnp.bfloat16
    )
    half = source.shape[0] // 2
    return picks[:half], picks[half:]


def swap_first(sent, axis):
    pairs = [(p * 2 + c, first_mate(p, c) * 2 + c) for p in RING for c in (0, 1)]
    return lax.ppermute(sent, (axis, "mp"), pairs)


def scatter_sums(streams, cuts, shapes):
    orders = [order for _, _, order in streams]
    sents, kepts = [], []
    for kept_parts, came_parts, _ in streams:
        rows = kept_parts[0].shape[0]
        cols = sum(part.shape[1] for part in kept_parts)
        sent, kept = whole(
            functools.partial(join_kernel, len(kept_parts)),
            [(rows // 2, cols)] * 2,
            jnp.bfloat16,
            *kept_parts,
            *came_parts,
        )
        sents.append(sent)
        kepts.append(kept)
    for turn in (1, 2):
        cames = stored(*(swap_first(sent, order[turn]) for sent, order in zip(sents, orders)))
        if turn == 2:
            break
        half = kepts[0].shape[0] // 2
        sents = [added(kept[:half], came[:half]) for kept, came in zip(kepts, cames)]
        kepts = [added(kept[half:], came[half:]) for kept, came in zip(kepts, cames)]
    pieces = jnp.concatenate(
        [added(kept, came).reshape(8, TILE, -1) for kept, came in zip(kepts, cames)], 2
    )
    (pieces,) = stored(pieces)
    came = lax.all_to_all(
        pieces,
        (*DP, "mp"),
        split_axis=0,
        concat_axis=0,
        tiled=True,
        axis_index_groups=cubes(second_mate),
    )
    return whole(functools.partial(sum_kernel, cuts), shapes, jnp.float32, came)


def per_device(
    tokens, sample_owner, sample_slot, teacher_cache, fc_weight, proj_weight, head_weight
):
    tok_rows, width = tokens.shape
    slots, patches, feats = teacher_cache.shape
    samples = tok_rows // patches
    devices = SIDE**3
    wide = -(-feats // 128) * 128
    loss_scale = 1.0 / math.sqrt(tok_rows * devices)
    core = lax.axis_index("mp")
    part = jnp.where(core == 0, tokens[:, : width // 2], tokens[:, width // 2 :])
    (part,) = stored(part)
    part = part.reshape(samples, patches, width // 2).transpose(1, 0, 2)
    part = lax.all_to_all(part, DP, split_axis=0, concat_axis=0, tiled=True)
    note = jnp.stack([sample_owner, sample_slot], 1).astype(jnp.bfloat16)
    note = jnp.pad(note, ((0, slots - samples), (0, wide - feats - 2)))
    part, message = stored(part, to_patch_major(teacher_cache, note))
    spread = lax.all_to_all(message, DP, split_axis=0, concat_axis=0, tiled=True)
    (target,) = whole(pick_kernel, [(devices * samples, wide)], jnp.bfloat16, spread)

    part = part.reshape(tok_rows, width // 2)
    other = swap_cores(part)
    tokens = jnp.concatenate(
        [jnp.where(core == 0, part, other), jnp.where(core == 0, other, part)], 1
    )
    tokens, core, head_weight = stored(tokens, core, head_weight)
    normal_in, _ = normalize(tokens)
    (normed_in,) = stored(normal_in.astype(jnp.bfloat16))
    pre_act = dot(normed_in, fc_weight)
    inner = jnp.tanh(gelu_coef * (pre_act + 0.044715 * pre_act**3))
    slope = 0.5 * (1.0 + inner) + 0.5 * pre_act * (1.0 - inner * inner) * gelu_coef * (
        1.0 + 3.0 * 0.044715 * pre_act * pre_act
    )
    act_out, slope = stored((0.5 * pre_act * (1.0 + inner)).astype(jnp.bfloat16), slope)
    (mlp_part,) = stored(dot(act_out, proj_weight).astype(jnp.bfloat16))
    mlp_out = mlp_part.astype(jnp.float32) + swap_cores(mlp_part).astype(jnp.float32)
    hidden = tokens.astype(jnp.float32) + mlp_out
    normal_out, inverse = normalize(hidden)
    normal_out, normed_out, inverse = stored(normal_out, normal_out.astype(jnp.bfloat16), inverse)
    head_wide = jnp.pad(head_weight, ((0, 0), (0, wide - feats)))
    (head_wide,) = stored(head_wide.T)
    (pred,) = stored(dot(normed_out, head_wide, 1, 1))

    orders = {"z": ("z", "x", "y"), "x": ("x", "y", "z"), "y": ("y", "z", "x")}
    picks = {axis: stored(*arranger(order, core)) for axis, order in orders.items()}
    head_cut, fc_cut, proj_cut = (640, 1152), 640, 640

    def turned(axes, half, values):
        return {
            axis: stored(dot(picks[axis][half], values, 1, 1).astype(jnp.bfloat16))[0]
            for axis in axes
        }

    def product(left, values):
        return dot(left, values).astype(jnp.bfloat16)

    head_left = [turned("zxy", half, normed_out) for half in (0, 1)]
    fc_left = [turned("zy", half, normed_in) for half in (0, 1)]

    (err_scaled,) = stored(
        ((pred - target.astype(jnp.float32)) * loss_scale).astype(jnp.bfloat16)
    )
    (grad_part,) = stored(dot(err_scaled, head_wide).astype(jnp.bfloat16))
    head_parts = {
        "z": err_scaled[:, : head_cut[0]],
        "x": err_scaled[:, head_cut[0] : head_cut[1]],
        "y": err_scaled[:, head_cut[1] :],
    }
    grad_came, *head_sents = stored(
        swap_cores(grad_part), *(product(head_left[0][axis], head_parts[axis]) for axis in "zxy")
    )
    head_came = {axis: swap_first(sent, axis) for axis, sent in zip("zxy", head_sents)}
    head_kept = {axis: product(head_left[1][axis], head_parts[axis]) for axis in "zxy"}
    grad_norm = grad_part.astype(jnp.float32) + grad_came.astype(jnp.float32)
    grad_hidden = inverse * (
        grad_norm
        - jnp.mean(grad_norm, axis=-1, keepdims=True)
        - normal_out * jnp.mean(grad_norm * normal_out, axis=-1, keepdims=True)
    )
    (grad_hidden,) = stored(grad_hidden.astype(jnp.bfloat16))
    (grad_pre,) = stored(
        (dot(grad_hidden, proj_weight, 1, 1) * slope).astype(jnp.bfloat16)
    )
    grad_pre, grad_hidden = stored(grad_pre, grad_hidden)
    fc_parts = {"z": grad_pre[:, :fc_cut], "y": grad_pre[:, fc_cut:]}
    proj_parts = {"z": act_out[:, :proj_cut], "x": act_out[:, proj_cut:]}
    proj_left = turned("zx", 0, grad_hidden)
    sents = {
        ("fc", "y"): product(fc_left[0]["y"], fc_parts["y"]),
        ("fc", "z"): product(fc_left[0]["z"], fc_parts["z"]),
        ("proj", "x"): product(proj_left["x"], proj_parts["x"]),
        ("proj", "z"): product(proj_left["z"], proj_parts["z"]),
    }
    sents = {key: stored(sent)[0] for key, sent in sents.items()}
    came = {
        key: swap_first(sent, key[1])
        for key, sent in sents.items()
    }
    fc_kept = {axis: product(fc_left[1][axis], fc_parts[axis]) for axis in "zy"}
    proj_left = turned("zx", 1, grad_hidden)
    proj_kept = {axis: product(proj_left[axis], proj_parts[axis]) for axis in "zx"}
    *head_cames, first, second, third, fourth = stored(*head_came.values(), *came.values())
    head_came = dict(zip(head_came, head_cames))
    came = dict(zip(came, (first, second, third, fourth)))
    streams = [
        (
            [head_kept["z"], fc_kept["z"], proj_kept["z"]],
            [head_came["z"], came["fc", "z"], came["proj", "z"]],
            orders["z"],
        ),
        ([head_kept["x"], proj_kept["x"]], [head_came["x"], came["proj", "x"]], orders["x"]),
        ([head_kept["y"], fc_kept["y"]], [head_came["y"], came["fc", "y"]], orders["y"]),
    ]
    units = fc_weight.shape[1]
    cuts = [
        (2, 0, head_cut[0]),
        (0, 0, fc_cut),
        (1, 0, proj_cut),
        (2, *head_cut),
        (1, proj_cut, units),
        (2, head_cut[1], wide),
        (0, fc_cut, units),
    ]
    fc_shard, proj_shard, head_shard = scatter_sums(
        streams, cuts, [(TILE, units), (TILE, units), (TILE, wide)]
    )
    return (fc_shard, proj_shard.T, head_shard[:, :feats])


def solution(mesh):
    torus = Mesh(mesh.devices.reshape(SIDE, SIDE, SIDE, 2), (*DP, "mp"))
    in_specs = (
        P(DP, None),
        P(DP),
        P(DP),
        P(DP, None, "mp"),
        P(None, "mp"),
        P("mp", None),
        P(None, "mp"),
    )
    out_specs = (P(DP, "mp"), P("mp", DP), P(DP, "mp"))
    return jax.shard_map(
        per_device, mesh=torus, in_specs=in_specs, out_specs=out_specs, check_vma=False
    )
```

```python
import functools
import math

import jax
import jax.numpy as jnp
from jax import lax
from jax.experimental import pallas as pl
from jax.experimental.pallas import tpu as pltpu
from jax.sharding import Mesh, PartitionSpec as P

gelu_coef = 0.7978845608
DP = ("z", "x", "y")
SIDE = 4
RING = list(range(SIDE))
TILE = 16


def normalize(values):
    values = values.astype(jnp.float32)
    center = jnp.mean(values, axis=-1, keepdims=True)
    spread = jnp.mean((values - center) ** 2, axis=-1, keepdims=True)
    inverse = 1.0 / jnp.sqrt(spread + 1e-06)
    return ((values - center) * inverse, inverse)


def dot(a, b, ca=1, cb=0):
    return lax.dot_general(a, b, (((ca,), (cb,)), ((), ())), preferred_element_type=jnp.float32)


def stored(*values):
    return lax.optimization_barrier(values)


def swap_cores(part):
    return lax.ppermute(part, "mp", [(0, 1), (1, 0)])


def spread_kernel(block_ref, note_ref, out_ref):
    slots, patches, feats = block_ref.shape
    rows = slots * patches
    to = lax.broadcasted_iota(jnp.int32, (rows, rows), 0)
    source = lax.broadcasted_iota(jnp.int32, (rows, rows), 1)
    pick = (source == (to % slots) * patches + to // slots).astype(jnp.bfloat16)
    moved = dot(pick, block_ref[...].reshape(rows, feats)).astype(jnp.bfloat16)
    out_ref[:, :, :feats] = moved.reshape(patches, slots, feats)
    note = note_ref[...]
    out_ref[:, :, feats:] = jnp.broadcast_to(note[None], (patches, *note.shape))


def to_patch_major(teacher_cache, note):
    slots, patches, feats = teacher_cache.shape
    wide = feats + note.shape[1]
    return pl.pallas_call(
        spread_kernel,
        grid=(patches // TILE,),
        in_specs=[
            pl.BlockSpec((slots, TILE, feats), lambda i: (0, i, 0)),
            pl.BlockSpec(note.shape, lambda i: (0, 0)),
        ],
        out_specs=pl.BlockSpec((TILE, slots, wide), lambda i: (i, 0, 0)),
        out_shape=jax.ShapeDtypeStruct((patches, slots, wide), jnp.bfloat16),
        compiler_params=pltpu.CompilerParams(vmem_limit_bytes=60 * 2**20),
    )(teacher_cache, note)


def pick_kernel(spread_ref, out_ref):
    devices, slots, wide = spread_ref.shape
    tok_rows = out_ref.shape[0]
    samples = tok_rows // devices
    note = spread_ref[:, :, wide - 128 :].astype(jnp.float32)[:, :samples, :].reshape(tok_rows, 128)
    column = (note[:, 64:65] * slots + note[:, 65:66]).astype(jnp.int32)
    blocks = lax.broadcasted_iota(jnp.int32, (tok_rows, devices * slots), 1)
    chosen = (column == blocks).astype(jnp.bfloat16)
    for start in range(0, wide, 512):
        cols = slice(start, min(start + 512, wide))
        rows = spread_ref[:, :, cols].reshape(devices * slots, cols.stop - start)
        out_ref[:, cols] = dot(chosen, rows).astype(jnp.bfloat16)


def added(left, right):
    return (left.astype(jnp.float32) + right.astype(jnp.float32)).astype(jnp.bfloat16)


def join_kernel(count, *refs):
    ins, (sent_ref, kept_ref) = refs[: 2 * count], refs[2 * count :]
    half = sent_ref.shape[0]
    start = 0
    for i in range(count):
        kept, came = ins[i], ins[count + i]
        cols = slice(start, start + kept.shape[1])
        sent_ref[:, cols] = added(kept[:half], came[:half])
        kept_ref[:, cols] = added(kept[half:], came[half:])
        start = cols.stop


def sum_kernel(cuts, came_ref, *out_refs):
    start = 0
    for name, first, last in cuts:
        cols = slice(start, start + last - first)
        total = came_ref[0, :, cols].astype(jnp.float32)
        for member in range(1, 8):
            total = total + came_ref[member, :, cols].astype(jnp.float32)
        out_refs[name][:, first:last] = total
        start = cols.stop


def whole(kernel, shapes, kind, *args):
    return pl.pallas_call(
        kernel,
        in_specs=[pl.BlockSpec(memory_space=pltpu.VMEM) for _ in args],
        out_specs=[pl.BlockSpec(memory_space=pltpu.VMEM) for _ in shapes],
        out_shape=[jax.ShapeDtypeStruct(shape, kind) for shape in shapes],
        compiler_params=pltpu.CompilerParams(vmem_limit_bytes=24 * 2**20),
    )(*args)


def first_mate(t, core):
    return t ^ 1 if core == 0 else 3 - t


def second_mate(t, core):
    return 3 - t if core == 0 else t ^ 1


def cubes(mate):
    groups = {}
    for core in (0, 1):
        for chip in range(SIDE**3):
            digits = (chip // SIDE**2, chip // SIDE % SIDE, chip % SIDE)
            sides = [sorted((t, mate(t, core))) for t in digits]
            group = tuple(
                ((z * SIDE + x) * SIDE + y) * 2 + core
                for z in sides[0]
                for x in sides[1]
                for y in sides[2]
            )
            groups[group] = True
    return [list(group) for group in groups]


def row_source(order, core):
    rows = jnp.arange(SIDE**3 * TILE, dtype=jnp.int32)
    source = rows % TILE
    for place, axis in enumerate(order):
        inner = 2 - DP.index(axis)
        t = lax.axis_index(axis)
        first = jnp.where(core == 0, t ^ 1, 3 - t)
        member = jnp.where(rows // (2 ** (5 - place) * TILE) % 2 == 0, first, t)
        second = jnp.where(core == 0, 3 - member, member ^ 1)
        digit = jnp.where(
            rows // (2**inner * TILE) % 2 == 0,
            jnp.minimum(member, second),
            jnp.maximum(member, second),
        )
        source = source + digit * (SIDE**inner * TILE)
    return source


def arranger(order, core):
    source = row_source(order, core)
    picks = (source[:, None] == jnp.arange(source.shape[0], dtype=jnp.int32)[None, :]).astype(
        jnp.bfloat16
    )
    half = source.shape[0] // 2
    return picks[:half], picks[half:]


def swap_first(sent, axis):
    pairs = [(p * 2 + c, first_mate(p, c) * 2 + c) for p in RING for c in (0, 1)]
    return lax.ppermute(sent, (axis, "mp"), pairs)


def scatter_sums(streams, cuts, shapes):
    orders = [order for _, _, order in streams]
    sents, kepts = [], []
    for kept_parts, came_parts, _ in streams:
        rows = kept_parts[0].shape[0]
        cols = sum(part.shape[1] for part in kept_parts)
        sent, kept = whole(
            functools.partial(join_kernel, len(kept_parts)),
            [(rows // 2, cols)] * 2,
            jnp.bfloat16,
            *kept_parts,
            *came_parts,
        )
        sents.append(sent)
        kepts.append(kept)
    for turn in (1, 2):
        cames = stored(*(swap_first(sent, order[turn]) for sent, order in zip(sents, orders)))
        if turn == 2:
            break
        half = kepts[0].shape[0] // 2
        sents = [added(kept[:half], came[:half]) for kept, came in zip(kepts, cames)]
        kepts = [added(kept[half:], came[half:]) for kept, came in zip(kepts, cames)]
    pieces = jnp.concatenate(
        [added(kept, came).reshape(8, TILE, -1) for kept, came in zip(kepts, cames)], 2
    )
    (pieces,) = stored(pieces)
    came = lax.all_to_all(
        pieces,
        (*DP, "mp"),
        split_axis=0,
        concat_axis=0,
        tiled=True,
        axis_index_groups=cubes(second_mate),
    )
    return whole(functools.partial(sum_kernel, cuts), shapes, jnp.float32, came)


def per_device(
    tokens, sample_owner, sample_slot, teacher_cache, fc_weight, proj_weight, head_weight
):
    tok_rows, width = tokens.shape
    slots, patches, feats = teacher_cache.shape
    samples = tok_rows // patches
    devices = SIDE**3
    wide = -(-feats // 128) * 128
    loss_scale = 1.0 / math.sqrt(tok_rows * devices)
    core = lax.axis_index("mp")
    part = jnp.where(core == 0, tokens[:, : width // 2], tokens[:, width // 2 :])
    (part,) = stored(part)
    part = part.reshape(samples, patches, width // 2).transpose(1, 0, 2)
    part = lax.all_to_all(part, DP, split_axis=0, concat_axis=0, tiled=True)
    note = jnp.stack([sample_owner, sample_slot], 1).astype(jnp.bfloat16)
    note = jnp.pad(note, ((0, slots - samples), (0, wide - feats - 2)))
    part, message = stored(part, to_patch_major(teacher_cache, note))
    spread = lax.all_to_all(message, DP, split_axis=0, concat_axis=0, tiled=True)
    (target,) = whole(pick_kernel, [(devices * samples, wide)], jnp.bfloat16, spread)

    part = part.reshape(tok_rows, width // 2)
    other = swap_cores(part)
    tokens = jnp.concatenate(
        [jnp.where(core == 0, part, other), jnp.where(core == 0, other, part)], 1
    )
    tokens, core, head_weight = stored(tokens, core, head_weight)
    normal_in, _ = normalize(tokens)
    (normed_in,) = stored(normal_in.astype(jnp.bfloat16))
    pre_act = dot(normed_in, fc_weight)
    inner = jnp.tanh(gelu_coef * (pre_act + 0.044715 * pre_act**3))
    slope = 0.5 * (1.0 + inner) + 0.5 * pre_act * (1.0 - inner * inner) * gelu_coef * (
        1.0 + 3.0 * 0.044715 * pre_act * pre_act
    )
    act_out, slope = stored((0.5 * pre_act * (1.0 + inner)).astype(jnp.bfloat16), slope)
    (mlp_part,) = stored(dot(act_out, proj_weight).astype(jnp.bfloat16))
    mlp_out = mlp_part.astype(jnp.float32) + swap_cores(mlp_part).astype(jnp.float32)
    hidden = tokens.astype(jnp.float32) + mlp_out
    normal_out, inverse = normalize(hidden)
    normal_out, normed_out, inverse = stored(normal_out, normal_out.astype(jnp.bfloat16), inverse)
    head_wide = jnp.pad(head_weight, ((0, 0), (0, wide - feats)))
    (head_wide,) = stored(head_wide.T)
    (pred,) = stored(dot(normed_out, head_wide, 1, 1))

    orders = {"z": ("z", "x", "y"), "x": ("x", "y", "z"), "y": ("y", "z", "x")}
    picks = {axis: stored(*arranger(order, core)) for axis, order in orders.items()}
    head_cut, fc_cut, proj_cut = (896, 1280), 512, 512

    def turned(axes, half, values):
        return {
            axis: stored(dot(picks[axis][half], values, 1, 1).astype(jnp.bfloat16))[0]
            for axis in axes
        }

    def product(left, values):
        return dot(left, values).astype(jnp.bfloat16)

    head_left = [turned("zxy", half, normed_out) for half in (0, 1)]
    fc_left = [turned("zy", half, normed_in) for half in (0, 1)]

    (err_scaled,) = stored(
        ((pred - target.astype(jnp.float32)) * loss_scale).astype(jnp.bfloat16)
    )
    (grad_part,) = stored(dot(err_scaled, head_wide).astype(jnp.bfloat16))
    head_parts = {
        "z": err_scaled[:, : head_cut[0]],
        "x": err_scaled[:, head_cut[0] : head_cut[1]],
        "y": err_scaled[:, head_cut[1] :],
    }
    grad_came, *head_sents = stored(
        swap_cores(grad_part), *(product(head_left[0][axis], head_parts[axis]) for axis in "zxy")
    )
    head_came = {axis: swap_first(sent, axis) for axis, sent in zip("zxy", head_sents)}
    head_kept = {axis: product(head_left[1][axis], head_parts[axis]) for axis in "zxy"}
    grad_norm = grad_part.astype(jnp.float32) + grad_came.astype(jnp.float32)
    grad_hidden = inverse * (
        grad_norm
        - jnp.mean(grad_norm, axis=-1, keepdims=True)
        - normal_out * jnp.mean(grad_norm * normal_out, axis=-1, keepdims=True)
    )
    (grad_hidden,) = stored(grad_hidden.astype(jnp.bfloat16))
    (grad_pre,) = stored(
        (dot(grad_hidden, proj_weight, 1, 1) * slope).astype(jnp.bfloat16)
    )
    grad_pre, grad_hidden = stored(grad_pre, grad_hidden)
    fc_parts = {"z": grad_pre[:, :fc_cut], "y": grad_pre[:, fc_cut:]}
    proj_parts = {"z": act_out[:, :proj_cut], "x": act_out[:, proj_cut:]}
    proj_left = turned("zx", 0, grad_hidden)
    sents = {
        ("fc", "y"): product(fc_left[0]["y"], fc_parts["y"]),
        ("fc", "z"): product(fc_left[0]["z"], fc_parts["z"]),
        ("proj", "x"): product(proj_left["x"], proj_parts["x"]),
        ("proj", "z"): product(proj_left["z"], proj_parts["z"]),
    }
    sents = {key: stored(sent)[0] for key, sent in sents.items()}
    came = {
        key: swap_first(sent, key[1])
        for key, sent in sents.items()
    }
    fc_kept = {axis: product(fc_left[1][axis], fc_parts[axis]) for axis in "zy"}
    proj_left = turned("zx", 1, grad_hidden)
    proj_kept = {axis: product(proj_left[axis], proj_parts[axis]) for axis in "zx"}
    *head_cames, first, second, third, fourth = stored(*head_came.values(), *came.values())
    head_came = dict(zip(head_came, head_cames))
    came = dict(zip(came, (first, second, third, fourth)))
    streams = [
        (
            [head_kept["z"], fc_kept["z"], proj_kept["z"]],
            [head_came["z"], came["fc", "z"], came["proj", "z"]],
            orders["z"],
        ),
        ([head_kept["x"], proj_kept["x"]], [head_came["x"], came["proj", "x"]], orders["x"]),
        ([head_kept["y"], fc_kept["y"]], [head_came["y"], came["fc", "y"]], orders["y"]),
    ]
    units = fc_weight.shape[1]
    cuts = [
        (2, 0, head_cut[0]),
        (0, 0, fc_cut),
        (1, 0, proj_cut),
        (2, *head_cut),
        (1, proj_cut, units),
        (2, head_cut[1], wide),
        (0, fc_cut, units),
    ]
    fc_shard, proj_shard, head_shard = scatter_sums(
        streams, cuts, [(TILE, units), (TILE, units), (TILE, wide)]
    )
    return (fc_shard, proj_shard.T, head_shard[:, :feats])


def solution(mesh):
    torus = Mesh(mesh.devices.reshape(SIDE, SIDE, SIDE, 2), (*DP, "mp"))
    in_specs = (
        P(DP, None),
        P(DP),
        P(DP),
        P(DP, None, "mp"),
        P(None, "mp"),
        P("mp", None),
        P(None, "mp"),
    )
    out_specs = (P(DP, "mp"), P("mp", DP), P(DP, "mp"))
    return jax.shard_map(
        per_device, mesh=torus, in_specs=in_specs, out_specs=out_specs, check_vma=False
    )
```

```python
import functools
import math

import jax
import jax.numpy as jnp
from jax import lax
from jax.experimental import pallas as pl
from jax.experimental.pallas import tpu as pltpu
from jax.sharding import Mesh, PartitionSpec as P

gelu_coef = 0.7978845608
DP = ("z", "x", "y")
SIDE = 4
RING = list(range(SIDE))
TILE = 16


def normalize(values):
    values = values.astype(jnp.float32)
    center = jnp.mean(values, axis=-1, keepdims=True)
    spread = jnp.mean((values - center) ** 2, axis=-1, keepdims=True)
    inverse = 1.0 / jnp.sqrt(spread + 1e-06)
    return ((values - center) * inverse, inverse)


def dot(a, b, ca=1, cb=0):
    return lax.dot_general(a, b, (((ca,), (cb,)), ((), ())), preferred_element_type=jnp.float32)


def stored(*values):
    return lax.optimization_barrier(values)


def swap_cores(part):
    return lax.ppermute(part, "mp", [(0, 1), (1, 0)])


def spread_kernel(block_ref, note_ref, out_ref):
    slots, patches, feats = block_ref.shape
    rows = slots * patches
    to = lax.broadcasted_iota(jnp.int32, (rows, rows), 0)
    source = lax.broadcasted_iota(jnp.int32, (rows, rows), 1)
    pick = (source == (to % slots) * patches + to // slots).astype(jnp.bfloat16)
    moved = dot(pick, block_ref[...].reshape(rows, feats)).astype(jnp.bfloat16)
    out_ref[:, :, :feats] = moved.reshape(patches, slots, feats)
    note = note_ref[...]
    out_ref[:, :, feats:] = jnp.broadcast_to(note[None], (patches, *note.shape))


def to_patch_major(teacher_cache, note):
    slots, patches, feats = teacher_cache.shape
    wide = feats + note.shape[1]
    return pl.pallas_call(
        spread_kernel,
        grid=(patches // TILE,),
        in_specs=[
            pl.BlockSpec((slots, TILE, feats), lambda i: (0, i, 0)),
            pl.BlockSpec(note.shape, lambda i: (0, 0)),
        ],
        out_specs=pl.BlockSpec((TILE, slots, wide), lambda i: (i, 0, 0)),
        out_shape=jax.ShapeDtypeStruct((patches, slots, wide), jnp.bfloat16),
        compiler_params=pltpu.CompilerParams(vmem_limit_bytes=60 * 2**20),
    )(teacher_cache, note)


def pick_kernel(spread_ref, out_ref):
    devices, slots, wide = spread_ref.shape
    tok_rows = out_ref.shape[0]
    samples = tok_rows // devices
    note = spread_ref[:, :, wide - 128 :].astype(jnp.float32)[:, :samples, :].reshape(tok_rows, 128)
    column = (note[:, 64:65] * slots + note[:, 65:66]).astype(jnp.int32)
    blocks = lax.broadcasted_iota(jnp.int32, (tok_rows, devices * slots), 1)
    chosen = (column == blocks).astype(jnp.bfloat16)
    for start in range(0, wide, 512):
        cols = slice(start, min(start + 512, wide))
        rows = spread_ref[:, :, cols].reshape(devices * slots, cols.stop - start)
        out_ref[:, cols] = dot(chosen, rows).astype(jnp.bfloat16)


def added(left, right):
    return (left.astype(jnp.float32) + right.astype(jnp.float32)).astype(jnp.bfloat16)


def join_kernel(count, *refs):
    ins, (sent_ref, kept_ref) = refs[: 2 * count], refs[2 * count :]
    half = sent_ref.shape[0]
    start = 0
    for i in range(count):
        kept, came = ins[i], ins[count + i]
        cols = slice(start, start + kept.shape[1])
        sent_ref[:, cols] = added(kept[:half], came[:half])
        kept_ref[:, cols] = added(kept[half:], came[half:])
        start = cols.stop


def sum_kernel(cuts, came_ref, *out_refs):
    start = 0
    for name, first, last in cuts:
        cols = slice(start, start + last - first)
        total = came_ref[0, :, cols].astype(jnp.float32)
        for member in range(1, 8):
            total = total + came_ref[member, :, cols].astype(jnp.float32)
        out_refs[name][:, first:last] = total
        start = cols.stop


def whole(kernel, shapes, kind, *args):
    return pl.pallas_call(
        kernel,
        in_specs=[pl.BlockSpec(memory_space=pltpu.VMEM) for _ in args],
        out_specs=[pl.BlockSpec(memory_space=pltpu.VMEM) for _ in shapes],
        out_shape=[jax.ShapeDtypeStruct(shape, kind) for shape in shapes],
        compiler_params=pltpu.CompilerParams(vmem_limit_bytes=24 * 2**20),
    )(*args)


def first_mate(t, core):
    return t ^ 1 if core == 0 else 3 - t


def second_mate(t, core):
    return 3 - t if core == 0 else t ^ 1


def cubes(mate):
    groups = {}
    for core in (0, 1):
        for chip in range(SIDE**3):
            digits = (chip // SIDE**2, chip // SIDE % SIDE, chip % SIDE)
            sides = [sorted((t, mate(t, core))) for t in digits]
            group = tuple(
                ((z * SIDE + x) * SIDE + y) * 2 + core
                for z in sides[0]
                for x in sides[1]
                for y in sides[2]
            )
            groups[group] = True
    return [list(group) for group in groups]


def row_source(order, core):
    rows = jnp.arange(SIDE**3 * TILE, dtype=jnp.int32)
    source = rows % TILE
    for place, axis in enumerate(order):
        inner = 2 - DP.index(axis)
        t = lax.axis_index(axis)
        first = jnp.where(core == 0, t ^ 1, 3 - t)
        member = jnp.where(rows // (2 ** (5 - place) * TILE) % 2 == 0, first, t)
        second = jnp.where(core == 0, 3 - member, member ^ 1)
        digit = jnp.where(
            rows // (2**inner * TILE) % 2 == 0,
            jnp.minimum(member, second),
            jnp.maximum(member, second),
        )
        source = source + digit * (SIDE**inner * TILE)
    return source


def arranger(order, core):
    source = row_source(order, core)
    picks = (source[:, None] == jnp.arange(source.shape[0], dtype=jnp.int32)[None, :]).astype(
        jnp.bfloat16
    )
    half = source.shape[0] // 2
    return picks[:half], picks[half:]


def swap_first(sent, axis):
    pairs = [(p * 2 + c, first_mate(p, c) * 2 + c) for p in RING for c in (0, 1)]
    return lax.ppermute(sent, (axis, "mp"), pairs)


def scatter_sums(streams, cuts, shapes):
    orders = [order for _, _, order in streams]
    sents, kepts = [], []
    for kept_parts, came_parts, _ in streams:
        rows = kept_parts[0].shape[0]
        cols = sum(part.shape[1] for part in kept_parts)
        sent, kept = whole(
            functools.partial(join_kernel, len(kept_parts)),
            [(rows // 2, cols)] * 2,
            jnp.bfloat16,
            *kept_parts,
            *came_parts,
        )
        sents.append(sent)
        kepts.append(kept)
    for turn in (1, 2):
        cames = stored(*(swap_first(sent, order[turn]) for sent, order in zip(sents, orders)))
        if turn == 2:
            break
        half = kepts[0].shape[0] // 2
        sents = [added(kept[:half], came[:half]) for kept, came in zip(kepts, cames)]
        kepts = [added(kept[half:], came[half:]) for kept, came in zip(kepts, cames)]
    pieces = jnp.concatenate(
        [added(kept, came).reshape(8, TILE, -1) for kept, came in zip(kepts, cames)], 2
    )
    (pieces,) = stored(pieces)
    came = lax.all_to_all(
        pieces,
        (*DP, "mp"),
        split_axis=0,
        concat_axis=0,
        tiled=True,
        axis_index_groups=cubes(second_mate),
    )
    return whole(functools.partial(sum_kernel, cuts), shapes, jnp.float32, came)


def per_device(
    tokens, sample_owner, sample_slot, teacher_cache, fc_weight, proj_weight, head_weight
):
    tok_rows, width = tokens.shape
    slots, patches, feats = teacher_cache.shape
    samples = tok_rows // patches
    devices = SIDE**3
    wide = -(-feats // 128) * 128
    loss_scale = 1.0 / math.sqrt(tok_rows * devices)
    core = lax.axis_index("mp")
    part = jnp.where(core == 0, tokens[:, : width // 2], tokens[:, width // 2 :])
    (part,) = stored(part)
    part = part.reshape(samples, patches, width // 2).transpose(1, 0, 2)
    part = lax.all_to_all(part, DP, split_axis=0, concat_axis=0, tiled=True)
    note = jnp.stack([sample_owner, sample_slot], 1).astype(jnp.bfloat16)
    note = jnp.pad(note, ((0, slots - samples), (0, wide - feats - 2)))
    part, message = stored(part, to_patch_major(teacher_cache, note))
    spread = lax.all_to_all(message, DP, split_axis=0, concat_axis=0, tiled=True)
    (target,) = whole(pick_kernel, [(devices * samples, wide)], jnp.bfloat16, spread)

    part = part.reshape(tok_rows, width // 2)
    other = swap_cores(part)
    tokens = jnp.concatenate(
        [jnp.where(core == 0, part, other), jnp.where(core == 0, other, part)], 1
    )
    tokens, core, head_weight = stored(tokens, core, head_weight)
    normal_in, _ = normalize(tokens)
    (normed_in,) = stored(normal_in.astype(jnp.bfloat16))
    pre_act = dot(normed_in, fc_weight)
    inner = jnp.tanh(gelu_coef * (pre_act + 0.044715 * pre_act**3))
    slope = 0.5 * (1.0 + inner) + 0.5 * pre_act * (1.0 - inner * inner) * gelu_coef * (
        1.0 + 3.0 * 0.044715 * pre_act * pre_act
    )
    act_out, slope = stored((0.5 * pre_act * (1.0 + inner)).astype(jnp.bfloat16), slope)
    (mlp_part,) = stored(dot(act_out, proj_weight).astype(jnp.bfloat16))
    mlp_out = mlp_part.astype(jnp.float32) + swap_cores(mlp_part).astype(jnp.float32)
    hidden = tokens.astype(jnp.float32) + mlp_out
    normal_out, inverse = normalize(hidden)
    normal_out, normed_out, inverse = stored(normal_out, normal_out.astype(jnp.bfloat16), inverse)
    head_wide = jnp.pad(head_weight, ((0, 0), (0, wide - feats)))
    (head_wide,) = stored(head_wide.T)
    (pred,) = stored(dot(normed_out, head_wide, 1, 1))

    orders = {"z": ("z", "x", "y"), "x": ("x", "y", "z"), "y": ("y", "z", "x")}
    picks = {axis: stored(*arranger(order, core)) for axis, order in orders.items()}
    head_cut, fc_cut, proj_cut = (1024, 1408), 384, 512

    def turned(axes, half, values):
        return {
            axis: stored(dot(picks[axis][half], values, 1, 1).astype(jnp.bfloat16))[0]
            for axis in axes
        }

    def product(left, values):
        return dot(left, values).astype(jnp.bfloat16)

    head_left = [turned("zxy", half, normed_out) for half in (0, 1)]
    fc_left = [turned("zy", half, normed_in) for half in (0, 1)]

    (err_scaled,) = stored(
        ((pred - target.astype(jnp.float32)) * loss_scale).astype(jnp.bfloat16)
    )
    (grad_part,) = stored(dot(err_scaled, head_wide).astype(jnp.bfloat16))
    head_parts = {
        "z": err_scaled[:, : head_cut[0]],
        "x": err_scaled[:, head_cut[0] : head_cut[1]],
        "y": err_scaled[:, head_cut[1] :],
    }
    grad_came, *head_sents = stored(
        swap_cores(grad_part), *(product(head_left[0][axis], head_parts[axis]) for axis in "zxy")
    )
    head_came = {axis: swap_first(sent, axis) for axis, sent in zip("zxy", head_sents)}
    head_kept = {axis: product(head_left[1][axis], head_parts[axis]) for axis in "zxy"}
    grad_norm = grad_part.astype(jnp.float32) + grad_came.astype(jnp.float32)
    grad_hidden = inverse * (
        grad_norm
        - jnp.mean(grad_norm, axis=-1, keepdims=True)
        - normal_out * jnp.mean(grad_norm * normal_out, axis=-1, keepdims=True)
    )
    (grad_hidden,) = stored(grad_hidden.astype(jnp.bfloat16))
    (grad_pre,) = stored(
        (dot(grad_hidden, proj_weight, 1, 1) * slope).astype(jnp.bfloat16)
    )
    grad_pre, grad_hidden = stored(grad_pre, grad_hidden)
    fc_parts = {"z": grad_pre[:, :fc_cut], "y": grad_pre[:, fc_cut:]}
    proj_parts = {"z": act_out[:, :proj_cut], "x": act_out[:, proj_cut:]}
    proj_left = turned("zx", 0, grad_hidden)
    sents = {
        ("fc", "y"): product(fc_left[0]["y"], fc_parts["y"]),
        ("fc", "z"): product(fc_left[0]["z"], fc_parts["z"]),
        ("proj", "x"): product(proj_left["x"], proj_parts["x"]),
        ("proj", "z"): product(proj_left["z"], proj_parts["z"]),
    }
    sents = {key: stored(sent)[0] for key, sent in sents.items()}
    came = {
        key: swap_first(sent, key[1])
        for key, sent in sents.items()
    }
    fc_kept = {axis: product(fc_left[1][axis], fc_parts[axis]) for axis in "zy"}
    proj_left = turned("zx", 1, grad_hidden)
    proj_kept = {axis: product(proj_left[axis], proj_parts[axis]) for axis in "zx"}
    *head_cames, first, second, third, fourth = stored(*head_came.values(), *came.values())
    head_came = dict(zip(head_came, head_cames))
    came = dict(zip(came, (first, second, third, fourth)))
    streams = [
        (
            [head_kept["z"], fc_kept["z"], proj_kept["z"]],
            [head_came["z"], came["fc", "z"], came["proj", "z"]],
            orders["z"],
        ),
        ([head_kept["x"], proj_kept["x"]], [head_came["x"], came["proj", "x"]], orders["x"]),
        ([head_kept["y"], fc_kept["y"]], [head_came["y"], came["fc", "y"]], orders["y"]),
    ]
    units = fc_weight.shape[1]
    cuts = [
        (2, 0, head_cut[0]),
        (0, 0, fc_cut),
        (1, 0, proj_cut),
        (2, *head_cut),
        (1, proj_cut, units),
        (2, head_cut[1], wide),
        (0, fc_cut, units),
    ]
    fc_shard, proj_shard, head_shard = scatter_sums(
        streams, cuts, [(TILE, units), (TILE, units), (TILE, wide)]
    )
    return (fc_shard, proj_shard.T, head_shard[:, :feats])


def solution(mesh):
    torus = Mesh(mesh.devices.reshape(SIDE, SIDE, SIDE, 2), (*DP, "mp"))
    in_specs = (
        P(DP, None),
        P(DP),
        P(DP),
        P(DP, None, "mp"),
        P(None, "mp"),
        P("mp", None),
        P(None, "mp"),
    )
    out_specs = (P(DP, "mp"), P("mp", DP), P(DP, "mp"))
    return jax.shard_map(
        per_device, mesh=torus, in_specs=in_specs, out_specs=out_specs, check_vma=False
    )
```
